32 devices in a mesh: dp: 4 (over z), ctx: 8 (over y, x, core).
Axes of the slice: x: 2, y: 2, z: 4, core: 2. Of those that a mesh axis runs over, the one named last changes fastest.
Arguments:
- queries: bfloat16 [4, 1024, 4096], P('dp', 'ctx'), may hold values from -216 to 216
- keys: bfloat16 [4, 1024, 1024], P('dp', 'ctx'), may hold values from -6 to 6
- values: bfloat16 [4, 1024, 1024], P('dp', 'ctx'), may hold values from -6 to 6
- out_grad: bfloat16 [4, 1024, 4096], P('dp', 'ctx'), may hold values from -6 to 6
- block_mask: int32 [32, 8, 8], replicated, may hold values from 0 to 1, as said below
Outputs:
- query_grad: bfloat16 [4, 1024, 4096], P('dp', 'ctx')
- key_grad: bfloat16 [4, 1024, 1024], P('dp', 'ctx')
- value_grad: bfloat16 [4, 1024, 1024], P('dp', 'ctx')
- z_loss: float32 [32], P('ctx')
The draws below stay inside these ranges and needn't reach their ends.
Inputs may be any that keep to these rules, and one draw needn't show every extreme that they name: block_mask[h, a, b] is 1 only where b <= a; block_mask[h, a, a] = 1 and block_mask[h, a, 0] = 1 for every head h and query block a.
All inputs are finite; a program needn't handle non-finite values.
Results may differ from the reference program's by a relative error of at most 0.014.
Values may be sent and summed in bfloat16 or wider, within the bound.
A program may use at most 128 MiB of HBM per device.

```python
import jax
import jax.numpy as jnp
from jax import lax

H = 32
KVH = 8
HD = 128
BLK = 128
SEQ = 1024
BATCH = 4


def query_key_pair(key):
    base = jax.random.fold_in(key, 101)
    query_key, key_key = jax.random.split(base, 2)
    key_raw = jnp.clip(jax.random.normal(key_key, (BATCH, SEQ, KVH, HD), jnp.float32), -6.0, 6.0)
    query_raw = jnp.clip(jax.random.normal(query_key, (BATCH, SEQ, H, HD), jnp.float32), -6.0, 6.0)
    key_out = key_raw
    query_out = query_raw
    return (query_out.reshape(BATCH, SEQ, H * HD), key_out.reshape(BATCH, SEQ, KVH * HD))


def draw_queries(key, part):
    return query_key_pair(key)[0].astype(jnp.bfloat16)


def draw_keys(key, part):
    return query_key_pair(key)[1].astype(jnp.bfloat16)


def draw_block_mask(key, part):
    block_total = SEQ // BLK
    level_key, column_key, slash_key = jax.random.split(jax.random.fold_in(key, 211), 3)
    level = jax.random.randint(level_key, (H, 1, 1), 1, 17)
    vertical = jax.random.randint(column_key, (H, 1, block_total), 0, 96) < level
    slash = jax.random.randint(slash_key, (H, block_total), 0, 384) < level[:, :, 0]
    query_block = jnp.arange(block_total)[:, None]
    key_block = jnp.arange(block_total)[None, :]
    offset = jnp.clip(query_block - key_block, 0, block_total - 1)
    slash_on = slash[:, offset]
    active = vertical | slash_on | (key_block == 0) | (key_block == query_block)
    active = active & (key_block <= query_block)
    return active.astype(jnp.int32)


def level_of(own_key, shape, cuts, smallest, high):
    factor_of = 1.0
    for dim, parts in cuts:
        draws = jax.random.uniform(jax.random.fold_in(jax.random.fold_in(own_key, 6), dim), (parts,), jnp.float32, smallest / len(cuts), high / len(cuts))
        factor_of = factor_of * jnp.repeat(jnp.exp(draws), shape[dim] // parts).reshape((-1,) + (1,) * (len(shape) - 1 - dim))
    return factor_of


def noise(own_key, dims, scale, bound, cuts=(), kind=jnp.bfloat16):
    result = jax.random.normal(own_key, dims, jnp.float32) * scale
    if len(cuts) > 0:
        result = level_of(own_key, dims, cuts, -0.22, 0.18) * result
    return jnp.clip(result, min=-bound, max=bound).astype(kind)


def setup_inputs(seed: int = 0) -> dict:
    arg_keys = jax.random.split(jax.random.key(seed), 6)
    return {
        "queries": draw_queries(jax.random.fold_in(arg_keys[5], 71), 0),
        "keys": draw_keys(jax.random.fold_in(arg_keys[5], 71), 0),
        "values": noise(arg_keys[2], (BATCH, SEQ, KVH * HD), 1.0, 6.0, ((0, 4), (1, 8))),
        "out_grad": noise(arg_keys[3], (BATCH, SEQ, H * HD), 1.0, 6.0, ((0, 4), (1, 8))),
        "block_mask": draw_block_mask(jax.random.fold_in(arg_keys[5], 71), 0),
    }


ZLOSS = 0.05
NEG = -1e30


def head_group(query_g, grad_g, key_g, value_g, mask_g):
    group_size = H // KVH
    tile_rows = 4 * BLK
    tile_count = SEQ // tile_rows
    softmax_scale = HD ** -0.5
    key_f32 = key_g.astype(jnp.float32)
    value_f32 = value_g.astype(jnp.float32)
    key_acc = jnp.zeros((SEQ, HD), jnp.float32)
    value_acc = jnp.zeros((SEQ, HD), jnp.float32)
    dq_heads = []
    z_heads = []
    for member in range(group_size):
        dq_tiles = []
        z_sum = jnp.zeros((), jnp.float32)
        for tile_pos in range(tile_count):
            first_row = tile_pos * tile_rows
            key_span = first_row + tile_rows
            q_tile = query_g[member, first_row:key_span].astype(jnp.float32)
            g_tile = grad_g[member, first_row:key_span].astype(jnp.float32)
            keys_here = key_f32[:key_span]
            values_here = value_f32[:key_span]
            scores = jnp.dot(q_tile, keys_here.T, precision=lax.Precision.HIGHEST) * softmax_scale
            tile_blocks = mask_g[member, 4 * tile_pos:4 * tile_pos + 4, :key_span // BLK]
            block_on = jnp.repeat(jnp.repeat(tile_blocks, BLK, axis=0), BLK, axis=1) > 0
            query_pos = first_row + jnp.arange(tile_rows)
            key_pos = jnp.arange(key_span)
            allowed = block_on & (key_pos[None, :] <= query_pos[:, None])
            row_max = jnp.max(jnp.where(allowed, scores, NEG), axis=1)
            row_sum = jnp.sum(jnp.where(allowed, jnp.exp(scores - row_max[:, None]), 0.0), axis=1)
            log_norm = row_max + jnp.log(row_sum)
            probs = jnp.where(allowed, jnp.exp(scores - log_norm[:, None]), 0.0)
            probs_low = probs.astype(jnp.bfloat16).astype(jnp.float32)
            attn_out = jnp.dot(probs_low, values_here, precision=lax.Precision.HIGHEST).astype(jnp.bfloat16)
            row_delta = jnp.sum(g_tile * attn_out.astype(jnp.float32), axis=1)
            prob_grad = jnp.dot(g_tile, values_here.T, precision=lax.Precision.HIGHEST)
            dscore = (probs * (prob_grad - row_delta[:, None] + 2.0 * ZLOSS * log_norm[:, None])).astype(jnp.bfloat16).astype(jnp.float32)
            dq_tile = softmax_scale * jnp.dot(dscore, keys_here, precision=lax.Precision.HIGHEST)
            dq_tiles.append(dq_tile.astype(jnp.bfloat16))
            key_acc = key_acc.at[:key_span].add(softmax_scale * jnp.dot(dscore.T, q_tile, precision=lax.Precision.HIGHEST))
            value_acc = value_acc.at[:key_span].add(jnp.dot(probs_low.T, g_tile, precision=lax.Precision.HIGHEST))
            z_sum = z_sum + jnp.sum(log_norm * log_norm)
        dq_heads.append(jnp.concatenate(dq_tiles, axis=0))
        z_heads.append(z_sum)
    return jnp.stack(dq_heads), key_acc.astype(jnp.bfloat16), value_acc.astype(jnp.bfloat16), jnp.stack(z_heads)


def reference(queries, keys, values, out_grad, block_mask):
    group_size = H // KVH
    block_total = SEQ // BLK
    query_g = queries.reshape(BATCH, SEQ, KVH, group_size, HD).transpose(0, 2, 3, 1, 4).reshape(BATCH * KVH, group_size, SEQ, HD)
    grad_g = out_grad.reshape(BATCH, SEQ, KVH, group_size, HD).transpose(0, 2, 3, 1, 4).reshape(BATCH * KVH, group_size, SEQ, HD)
    key_g = keys.reshape(BATCH, SEQ, KVH, HD).transpose(0, 2, 1, 3).reshape(BATCH * KVH, SEQ, HD)
    value_g = values.reshape(BATCH, SEQ, KVH, HD).transpose(0, 2, 1, 3).reshape(BATCH * KVH, SEQ, HD)
    mask_g = jnp.tile(block_mask.reshape(KVH, group_size, block_total, block_total), (BATCH, 1, 1, 1))

    def run_group(pieces):
        return head_group(pieces[0], pieces[1], pieces[2], pieces[3], pieces[4])

    dq_all, dk_all, dv_all, z_all = lax.map(run_group, (query_g, grad_g, key_g, value_g, mask_g))
    query_grad = dq_all.reshape(BATCH, KVH, group_size, SEQ, HD).transpose(0, 3, 1, 2, 4).reshape(BATCH, SEQ, H * HD)
    key_grad = dk_all.reshape(BATCH, KVH, SEQ, HD).transpose(0, 2, 1, 3).reshape(BATCH, SEQ, KVH * HD)
    value_grad = dv_all.reshape(BATCH, KVH, SEQ, HD).transpose(0, 2, 1, 3).reshape(BATCH, SEQ, KVH * HD)
    z_loss = jnp.sum(z_all.reshape(BATCH, H), axis=0) * (ZLOSS / (BATCH * SEQ))
    return query_grad, key_grad, value_grad, z_loss
```

```python
import functools
import math

import jax
import jax.numpy as jnp
from jax import lax
from jax.experimental import pallas as pl
from jax.experimental.pallas import tpu as pltpu
from jax.sharding import PartitionSpec as P

H = 32
KVH = 8
HD = 128
BLK = 128
ZLOSS = 0.05
NEG = -1e30
TILE = 2 * BLK
MESH = pl.DeviceIdType.MESH
LOG2E = math.log2(math.e)
LN2 = math.log(2.0)


def dot(a, b):
    return jnp.dot(a, b, preferred_element_type=jnp.float32)


def steps(count, step, state):
    if isinstance(count, int) and count <= 4:
        for i in range(count):
            state = step(i, state)
        return state
    return lax.fori_loop(0, count, step, state)


def rows(i, size):
    return pl.ds(i * size if isinstance(i, int) else pl.multiple_of(i * size, size), size)


def fold(x, op):
    return op(x.reshape(x.shape[0] // 8, 8, x.shape[1]), axis=0)


def kernel(
    sizes,
    mask, q_in, g_in, k_in, v_in,
    dq_out, dk_out, dv_out, z_out,
    q_all, g_all, k_all, v_all, k_tr, v_tr,
    score, dk_acc, dv_acc, dq_buf, dk_buf, dv_buf, z_own, z_all,
    q_sem, g_sem, kv_sem, out_sem, send_sem, z_sem,
):
    n, dp, per, share, tok = sizes
    seq = n * tok
    tiles = seq // TILE
    me = lax.axis_index("ctx")
    my_dp = lax.axis_index("dp")
    group = H // KVH
    scale = HD ** (-0.5)

    barrier = pltpu.get_barrier_semaphore()

    def greet(j, c):
        pl.semaphore_signal(
            barrier, inc=1, device_id=(my_dp, lax.rem(me + j, n)), device_id_type=MESH
        )
        return c

    def greet_dp(j, c):
        pl.semaphore_signal(
            barrier, inc=1, device_id=(lax.rem(my_dp + j, dp), me), device_id_type=MESH
        )
        return c

    lax.fori_loop(1, n, greet, 0)
    lax.fori_loop(1, dp, greet_dp, 0)
    pl.semaphore_wait(barrier, n - 1 + dp - 1)

    def lanes(i):
        return pl.ds(pl.multiple_of(i * HD, HD), HD)

    def remote(src, dst, send, recv, target):
        pltpu.make_async_remote_copy(
            src_ref=src, dst_ref=dst, send_sem=send, recv_sem=recv,
            device_id=(my_dp, target), device_id_type=MESH,
        ).start()

    mine = rows(me, tok)

    def kv_head(device):
        return (device * per) // group

    def send_kv(j, c):
        to = lax.rem(me + j, n)
        col = lanes(kv_head(to))
        remote(k_in.at[0, :, col], k_all.at[mine], send_sem.at[0], kv_sem.at[0], to)
        remote(v_in.at[0, :, col], v_all.at[mine], send_sem.at[1], kv_sem.at[1], to)
        return c

    lax.fori_loop(1, n, send_kv, 0)
    own = lanes(kv_head(me))
    pltpu.make_async_copy(k_in.at[0, :, own], k_all.at[mine], kv_sem.at[0]).start()
    pltpu.make_async_copy(v_in.at[0, :, own], v_all.at[mine], kv_sem.at[1]).start()

    def send_head(h, c):
        def send_q(j, c):
            to = lax.rem(me + j, n)
            col = lanes(to * per + h)
            remote(q_in.at[0, :, col], q_all.at[h, mine], send_sem.at[2], q_sem.at[h], to)
            remote(g_in.at[0, :, col], g_all.at[h, mine], send_sem.at[3], g_sem.at[h], to)
            return c

        lax.fori_loop(1, n, send_q, 0)
        col = lanes(me * per + h)
        pltpu.make_async_copy(q_in.at[0, :, col], q_all.at[h, mine], q_sem.at[h]).start()
        pltpu.make_async_copy(g_in.at[0, :, col], g_all.at[h, mine], g_sem.at[h]).start()
        return c

    lax.fori_loop(0, per, send_head, 0)

    def wait_for(ref, sem):
        pltpu.make_async_copy(ref, ref, sem).wait()

    z_own[...] = jnp.zeros_like(z_own)
    dk_acc[...] = jnp.zeros_like(dk_acc)
    dv_acc[...] = jnp.zeros_like(dv_acc)
    wait_for(k_all, kv_sem.at[0])
    wait_for(v_all, kv_sem.at[1])

    def turn(c, s):
        at = rows(c, TILE)
        k_tr[:, at] = k_all[at].astype(jnp.float32).T.astype(jnp.bfloat16)
        v_tr[:, at] = v_all[at].astype(jnp.float32).T.astype(jnp.bfloat16)
        return s

    steps(tiles, turn, 0)
    first_half = lax.broadcasted_iota(jnp.int32, (1, TILE), 1) < BLK
    causal = lax.broadcasted_iota(jnp.int32, (TILE, TILE), 0) <= lax.broadcasted_iota(
        jnp.int32, (TILE, TILE), 1
    )

    def one_head(h, c):
        wait_for(q_all.at[h], q_sem.at[h])
        wait_for(g_all.at[h], g_sem.at[h])
        head = me * per + h

        def one_tile(t):
            q_at = rows(t, TILE)
            q = q_all[h, q_at, :]
            g = g_all[h, q_at, :]
            q_tr = q.astype(jnp.float32).T.astype(jnp.bfloat16)
            g_f32 = g.astype(jnp.float32).T
            g_tr = g_f32.astype(jnp.bfloat16)

            def bias(c):
                parts = []
                for b in range(2):
                    left = mask[head, 2 * t, 2 * c + b]
                    right = mask[head, 2 * t + 1, 2 * c + b]
                    on = jnp.where(first_half, left, right).astype(jnp.float32)
                    parts.append(jnp.broadcast_to((1.0 - on) * NEG, (BLK, TILE)))
                return jnp.concatenate(parts, axis=0)

            def score_chunk(c, top, diagonal):
                at = rows(c, TILE)
                s = dot(k_all[at], q_tr) * (scale * LOG2E) + bias(c)
                if diagonal:
                    s = jnp.where(causal, s, NEG)
                score[at] = s
                return jnp.maximum(top, fold(s, jnp.max))

            top = jnp.full((8, TILE), NEG, jnp.float32)
            top = steps(t, lambda c, x: score_chunk(c, x, False), top)
            top = score_chunk(t, top, True)
            top = jnp.max(top, axis=0, keepdims=True)

            def exp_chunk(c, state):
                total, out = state
                at = rows(c, TILE)
                e = jnp.exp2(score[at] - top)
                score[at] = e
                out = out + dot(v_tr[:, at], e.astype(jnp.bfloat16))
                return total + fold(e, jnp.sum), out

            total, out = steps(
                t + 1, exp_chunk,
                (jnp.zeros((8, TILE), jnp.float32), jnp.zeros((HD, TILE), jnp.float32)),
            )
            total = jnp.sum(total, axis=0, keepdims=True)
            inverse = 1.0 / total
            out = (out * inverse).astype(jnp.bfloat16).astype(jnp.float32)
            delta = jnp.sum(g_f32 * out, axis=0, keepdims=True)
            log_norm = top * LN2 + jnp.log(total)
            shift = delta - (2.0 * ZLOSS) * log_norm
            square = log_norm * log_norm
            z_own[pl.ds(h, 1), :] += square[:, :BLK] + square[:, BLK:]

            def grad_chunk(c, dq):
                at = rows(c, TILE)
                p = score[at] * inverse
                dv_acc[at] += dot(p.astype(jnp.bfloat16), g)
                ds = (p * (dot(v_all[at], g_tr) - shift)).astype(jnp.bfloat16)
                dk_acc[at] += dot(ds, q)
                return dq + dot(k_tr[:, at], ds)

            dq = steps(t + 1, grad_chunk, jnp.zeros((HD, TILE), jnp.float32))
            dq_buf[h, q_at, :] = (dq * scale).T.astype(jnp.bfloat16)

            for part in range(TILE // tok):
                to = t * (TILE // tok) + part
                src = dq_buf.at[h, rows(to, tok)]
                dst = dq_out.at[0, :, lanes(head)]

                @pl.when(me == to)
                def _():
                    pltpu.make_async_copy(src, dst, out_sem.at[0]).start()

                @pl.when(me != to)
                def _():
                    remote(src, dst, send_sem.at[4], out_sem.at[0], to)

            @pl.when(h == per - 1)
            def _():
                dk_buf[q_at] = (dk_acc[q_at] * scale).astype(jnp.bfloat16)
                dv_buf[q_at] = dv_acc[q_at].astype(jnp.bfloat16)
                slot = lax.rem(me, share)
                col = lanes(kv_head(me))
                for part in range(TILE // tok):
                    to = t * (TILE // tok) + part
                    src_k = dk_buf.at[rows(to, tok)]
                    src_v = dv_buf.at[rows(to, tok)]

                    @pl.when(me == to)
                    def _():
                        pltpu.make_async_copy(src_k, dk_out.at[slot, :, col], out_sem.at[1]).start()
                        pltpu.make_async_copy(src_v, dv_out.at[slot, :, col], out_sem.at[2]).start()

                    @pl.when(me != to)
                    def _():
                        remote(src_k, dk_out.at[slot, :, col], send_sem.at[5], out_sem.at[1], to)
                        remote(src_v, dv_out.at[slot, :, col], send_sem.at[6], out_sem.at[2], to)

        if tiles <= 4:
            for t in reversed(range(tiles)):
                one_tile(t)
        else:
            def tile_step(i, s):
                one_tile(tiles - 1 - i)
                return s

            lax.fori_loop(0, tiles, tile_step, 0)
        return c

    lax.fori_loop(0, per, one_head, 0)

    pltpu.make_async_copy(z_own, z_all.at[my_dp], z_sem.at[1]).start()

    def send_z(j, c):
        pltpu.make_async_remote_copy(
            src_ref=z_own, dst_ref=z_all.at[my_dp], send_sem=z_sem.at[0], recv_sem=z_sem.at[1],
            device_id=(lax.rem(my_dp + j, dp), me), device_id_type=MESH,
        ).start()
        return c

    lax.fori_loop(1, dp, send_z, 0)
    wait_for(z_all, z_sem.at[1])
    z_sum = jnp.sum(jnp.sum(z_all[...], axis=0), axis=1, keepdims=True)
    z_out[...] = jnp.broadcast_to(z_sum * (ZLOSS / (seq * dp)), z_out.shape)

    wait_for(dq_out, out_sem.at[0])
    wait_for(dk_out, out_sem.at[1])
    wait_for(dv_out, out_sem.at[2])
    others = pl.ds(0, seq - tok)
    wide = pl.ds(0, (n - 1) * per * HD)
    wait_for(k_all.at[others], send_sem.at[0])
    wait_for(v_all.at[others], send_sem.at[1])
    wait_for(q_in.at[0, :, wide], send_sem.at[2])
    wait_for(g_in.at[0, :, wide], send_sem.at[3])
    wait_for(dq_out.at[0, :, wide], send_sem.at[4])
    wait_for(dk_buf.at[others], send_sem.at[5])
    wait_for(dv_buf.at[others], send_sem.at[6])
    wait_for(z_all.at[pl.ds(0, dp - 1)], z_sem.at[0])


def body(queries, keys, values, out_grad, block_mask):
    tok = queries.shape[1]
    n = lax.axis_size("ctx")
    dp = lax.axis_size("dp")
    per = H // n
    share = max(1, n // KVH)
    seq = tok * n
    low, wide = jnp.bfloat16, jnp.float32
    anywhere = pl.BlockSpec(memory_space=pl.ANY)
    dq, dk, dv, z = pl.pallas_call(
        functools.partial(kernel, (n, dp, per, share, tok)),
        out_shape=(
            jax.ShapeDtypeStruct(queries.shape, low),
            jax.ShapeDtypeStruct((share, tok, KVH * HD), low),
            jax.ShapeDtypeStruct((share, tok, KVH * HD), low),
            jax.ShapeDtypeStruct((8, BLK), wide),
        ),
        in_specs=[pl.BlockSpec(memory_space=pltpu.SMEM)] + [anywhere] * 4,
        out_specs=(anywhere, anywhere, anywhere, pl.BlockSpec(memory_space=pltpu.VMEM)),
        scratch_shapes=[
            pltpu.VMEM((per, seq, HD), low),
            pltpu.VMEM((per, seq, HD), low),
            pltpu.VMEM((seq, HD), low),
            pltpu.VMEM((seq, HD), low),
            pltpu.VMEM((HD, seq), low),
            pltpu.VMEM((HD, seq), low),
            pltpu.VMEM((seq, TILE), wide),
            pltpu.VMEM((seq, HD), wide),
            pltpu.VMEM((seq, HD), wide),
            pltpu.VMEM((per, seq, HD), low),
            pltpu.VMEM((seq, HD), low),
            pltpu.VMEM((seq, HD), low),
            pltpu.VMEM((8, BLK), wide),
            pltpu.VMEM((dp, 8, BLK), wide),
            pltpu.SemaphoreType.DMA((per,)),
            pltpu.SemaphoreType.DMA((per,)),
            pltpu.SemaphoreType.DMA((2,)),
            pltpu.SemaphoreType.DMA((3,)),
            pltpu.SemaphoreType.DMA((7,)),
            pltpu.SemaphoreType.DMA((2,)),
        ],
        compiler_params=pltpu.CompilerParams(
            collective_id=0, has_side_effects=True, vmem_limit_bytes=48 * 1024 * 1024
        ),
        name="attention_exchange",
    )(block_mask, queries, out_grad, keys, values)
    if share > 1:
        dk = jnp.sum(dk.astype(wide), axis=0, keepdims=True).astype(low)
        dv = jnp.sum(dv.astype(wide), axis=0, keepdims=True).astype(low)
    return (dq, dk, dv, z[:per, 0])


def solution(mesh):
    return jax.shard_map(
        body,
        mesh=mesh,
        in_specs=(
            P("dp", "ctx", None),
            P("dp", "ctx", None),
            P("dp", "ctx", None),
            P("dp", "ctx", None),
            P(),
        ),
        out_specs=(P("dp", "ctx", None), P("dp", "ctx", None), P("dp", "ctx", None), P("ctx")),
        check_vma=False,
    )
```

```python
import functools
import math

import jax
import jax.numpy as jnp
from jax import lax
from jax.experimental import pallas as pl
from jax.experimental.pallas import tpu as pltpu
from jax.sharding import PartitionSpec as P

H = 32
KVH = 8
HD = 128
BLK = 128
ZLOSS = 0.05
NEG = -1e30
TILE = 2 * BLK
MESH = pl.DeviceIdType.MESH
LOG2E = math.log2(math.e)
LN2 = math.log(2.0)


def dot(a, b):
    return jnp.dot(a, b, preferred_element_type=jnp.float32)


def steps(count, step, state):
    if isinstance(count, int) and count <= 4:
        for i in range(count):
            state = step(i, state)
        return state
    return lax.fori_loop(0, count, step, state)


def rows(i, size):
    return pl.ds(i * size if isinstance(i, int) else pl.multiple_of(i * size, size), size)


def fold(x, op):
    return op(x.reshape(x.shape[0] // 8, 8, x.shape[1]), axis=0)


def kernel(
    sizes,
    mask, q_in, g_in, k_in, v_in,
    dq_out, dk_out, dv_out, z_out,
    q_all, g_all, k_all, v_all, k_tr, v_tr,
    score, dk_acc, dv_acc, dq_buf, dk_buf, dv_buf, z_own, z_all,
    q_sem, g_sem, kv_sem, out_sem, send_sem, z_sem,
):
    n, dp, per, share, tok = sizes
    seq = n * tok
    tiles = seq // TILE
    me = lax.axis_index("ctx")
    my_dp = lax.axis_index("dp")
    group = H // KVH
    scale = HD ** (-0.5)

    barrier = pltpu.get_barrier_semaphore()

    def greet(j, c):
        pl.semaphore_signal(
            barrier, inc=1, device_id=(my_dp, lax.rem(me + j, n)), device_id_type=MESH
        )
        return c

    def greet_dp(j, c):
        pl.semaphore_signal(
            barrier, inc=1, device_id=(lax.rem(my_dp + j, dp), me), device_id_type=MESH
        )
        return c

    lax.fori_loop(1, n, greet, 0)
    lax.fori_loop(1, dp, greet_dp, 0)
    pl.semaphore_wait(barrier, n - 1 + dp - 1)

    def lanes(i):
        return pl.ds(pl.multiple_of(i * HD, HD), HD)

    def remote(src, dst, send, recv, target):
        pltpu.make_async_remote_copy(
            src_ref=src, dst_ref=dst, send_sem=send, recv_sem=recv,
            device_id=(my_dp, target), device_id_type=MESH,
        ).start()

    mine = rows(me, tok)

    def kv_head(device):
        return (device * per) // group

    def send_kv(j, c):
        to = lax.rem(me + j, n)
        col = lanes(kv_head(to))
        remote(k_in.at[0, :, col], k_all.at[mine], send_sem.at[0], kv_sem.at[0], to)
        remote(v_in.at[0, :, col], v_all.at[mine], send_sem.at[1], kv_sem.at[1], to)
        return c

    lax.fori_loop(1, n, send_kv, 0)
    own = lanes(kv_head(me))
    pltpu.make_async_copy(k_in.at[0, :, own], k_all.at[mine], kv_sem.at[0]).start()
    pltpu.make_async_copy(v_in.at[0, :, own], v_all.at[mine], kv_sem.at[1]).start()

    def send_head(h, c):
        def send_q(j, c):
            to = lax.rem(me + j, n)
            col = lanes(to * per + h)
            remote(q_in.at[0, :, col], q_all.at[h, mine], send_sem.at[2], q_sem.at[h], to)
            remote(g_in.at[0, :, col], g_all.at[h, mine], send_sem.at[3], g_sem.at[h], to)
            return c

        lax.fori_loop(1, n, send_q, 0)
        col = lanes(me * per + h)
        pltpu.make_async_copy(q_in.at[0, :, col], q_all.at[h, mine], q_sem.at[h]).start()
        pltpu.make_async_copy(g_in.at[0, :, col], g_all.at[h, mine], g_sem.at[h]).start()
        return c

    lax.fori_loop(0, per, send_head, 0)

    def wait_for(ref, sem):
        pltpu.make_async_copy(ref, ref, sem).wait()

    z_own[...] = jnp.zeros_like(z_own)
    dk_acc[...] = jnp.zeros_like(dk_acc)
    dv_acc[...] = jnp.zeros_like(dv_acc)
    wait_for(k_all, kv_sem.at[0])
    wait_for(v_all, kv_sem.at[1])

    def turn(c, s):
        at = rows(c, TILE)
        k_tr[:, at] = k_all[at].astype(jnp.float32).T.astype(jnp.bfloat16)
        v_tr[:, at] = v_all[at].astype(jnp.float32).T.astype(jnp.bfloat16)
        return s

    steps(tiles, turn, 0)
    first_half = lax.broadcasted_iota(jnp.int32, (1, TILE), 1) < BLK
    causal = lax.broadcasted_iota(jnp.int32, (TILE, TILE), 0) <= lax.broadcasted_iota(
        jnp.int32, (TILE, TILE), 1
    )

    def one_head(h, c):
        wait_for(q_all.at[h], q_sem.at[h])
        wait_for(g_all.at[h], g_sem.at[h])
        head = me * per + h

        def one_tile(t):
            q_at = rows(t, TILE)
            q = q_all[h, q_at, :]
            g = g_all[h, q_at, :]
            q_tr = q.astype(jnp.float32).T.astype(jnp.bfloat16)
            g_f32 = g.astype(jnp.float32).T
            g_tr = g_f32.astype(jnp.bfloat16)

            def bias(c):
                parts = []
                for b in range(2):
                    left = mask[2 * t, 2 * c + b, head]
                    right = mask[2 * t + 1, 2 * c + b, head]
                    on = jnp.where(first_half, left, right).astype(jnp.float32)
                    parts.append(jnp.broadcast_to((1.0 - on) * NEG, (BLK, TILE)))
                return jnp.concatenate(parts, axis=0)

            def score_chunk(c, top, diagonal):
                at = rows(c, TILE)
                s = dot(k_all[at], q_tr) * (scale * LOG2E) + bias(c)
                if diagonal:
                    s = jnp.where(causal, s, NEG)
                score[at] = s
                return jnp.maximum(top, fold(s, jnp.max))

            top = jnp.full((8, TILE), NEG, jnp.float32)
            top = steps(t, lambda c, x: score_chunk(c, x, False), top)
            top = score_chunk(t, top, True)
            top = jnp.max(top, axis=0, keepdims=True)

            def exp_chunk(c, state):
                total, out = state
                at = rows(c, TILE)
                e = jnp.exp2(score[at] - top)
                score[at] = e
                out = out + dot(v_tr[:, at], e.astype(jnp.bfloat16))
                return total + fold(e, jnp.sum), out

            total, out = steps(
                t + 1, exp_chunk,
                (jnp.zeros((8, TILE), jnp.float32), jnp.zeros((HD, TILE), jnp.float32)),
            )
            total = jnp.sum(total, axis=0, keepdims=True)
            inverse = 1.0 / total
            out = (out * inverse).astype(jnp.bfloat16).astype(jnp.float32)
            delta = jnp.sum(g_f32 * out, axis=0, keepdims=True)
            log_norm = top * LN2 + jnp.log(total)
            shift = delta - (2.0 * ZLOSS) * log_norm
            square = log_norm * log_norm
            z_own[pl.ds(h, 1), :] += square[:, :BLK] + square[:, BLK:]

            def grad_chunk(c, dq):
                at = rows(c, TILE)
                p = score[at] * inverse
                dv_acc[at] += dot(p.astype(jnp.bfloat16), g)
                ds = (p * (dot(v_all[at], g_tr) - shift)).astype(jnp.bfloat16)
                dk_acc[at] += dot(ds, q)
                return dq + dot(k_tr[:, at], ds)

            dq = steps(t + 1, grad_chunk, jnp.zeros((HD, TILE), jnp.float32))
            dq_buf[h, q_at, :] = (dq * scale).T.astype(jnp.bfloat16)

            for part in range(TILE // tok):
                to = t * (TILE // tok) + part
                src = dq_buf.at[h, rows(to, tok)]
                dst = dq_out.at[0, :, lanes(head)]

                @pl.when(me == to)
                def _():
                    pltpu.make_async_copy(src, dst, out_sem.at[0]).start()

                @pl.when(me != to)
                def _():
                    remote(src, dst, send_sem.at[4], out_sem.at[0], to)

            @pl.when(h == per - 1)
            def _():
                dk_buf[q_at] = (dk_acc[q_at] * scale).astype(jnp.bfloat16)
                dv_buf[q_at] = dv_acc[q_at].astype(jnp.bfloat16)
                slot = lax.rem(me, share)
                col = lanes(kv_head(me))
                for part in range(TILE // tok):
                    to = t * (TILE // tok) + part
                    src_k = dk_buf.at[rows(to, tok)]
                    src_v = dv_buf.at[rows(to, tok)]

                    @pl.when(me == to)
                    def _():
                        pltpu.make_async_copy(src_k, dk_out.at[slot, :, col], out_sem.at[1]).start()
                        pltpu.make_async_copy(src_v, dv_out.at[slot, :, col], out_sem.at[2]).start()

                    @pl.when(me != to)
                    def _():
                        remote(src_k, dk_out.at[slot, :, col], send_sem.at[5], out_sem.at[1], to)
                        remote(src_v, dv_out.at[slot, :, col], send_sem.at[6], out_sem.at[2], to)

        if tiles <= 4:
            for t in reversed(range(tiles)):
                one_tile(t)
        else:
            def tile_step(i, s):
                one_tile(tiles - 1 - i)
                return s

            lax.fori_loop(0, tiles, tile_step, 0)
        return c

    lax.fori_loop(0, per, one_head, 0)

    pltpu.make_async_copy(z_own, z_all.at[my_dp], z_sem.at[1]).start()

    def send_z(j, c):
        pltpu.make_async_remote_copy(
            src_ref=z_own, dst_ref=z_all.at[my_dp], send_sem=z_sem.at[0], recv_sem=z_sem.at[1],
            device_id=(lax.rem(my_dp + j, dp), me), device_id_type=MESH,
        ).start()
        return c

    lax.fori_loop(1, dp, send_z, 0)
    wait_for(z_all, z_sem.at[1])
    z_sum = jnp.sum(jnp.sum(z_all[...], axis=0), axis=1, keepdims=True)
    z_out[...] = jnp.broadcast_to(z_sum * (ZLOSS / (seq * dp)), z_out.shape)

    wait_for(dq_out, out_sem.at[0])
    wait_for(dk_out, out_sem.at[1])
    wait_for(dv_out, out_sem.at[2])
    others = pl.ds(0, seq - tok)
    wide = pl.ds(0, (n - 1) * per * HD)
    wait_for(k_all.at[others], send_sem.at[0])
    wait_for(v_all.at[others], send_sem.at[1])
    wait_for(q_in.at[0, :, wide], send_sem.at[2])
    wait_for(g_in.at[0, :, wide], send_sem.at[3])
    wait_for(dq_out.at[0, :, wide], send_sem.at[4])
    wait_for(dk_buf.at[others], send_sem.at[5])
    wait_for(dv_buf.at[others], send_sem.at[6])
    wait_for(z_all.at[pl.ds(0, dp - 1)], z_sem.at[0])


def body(queries, keys, values, out_grad, block_mask):
    tok = queries.shape[1]
    n = lax.axis_size("ctx")
    dp = lax.axis_size("dp")
    per = H // n
    share = max(1, n // KVH)
    seq = tok * n
    low, wide = jnp.bfloat16, jnp.float32
    anywhere = pl.BlockSpec(memory_space=pl.ANY)
    dq, dk, dv, z = pl.pallas_call(
        functools.partial(kernel, (n, dp, per, share, tok)),
        out_shape=(
            jax.ShapeDtypeStruct(queries.shape, low),
            jax.ShapeDtypeStruct((share, tok, KVH * HD), low),
            jax.ShapeDtypeStruct((share, tok, KVH * HD), low),
            jax.ShapeDtypeStruct((8, BLK), wide),
        ),
        in_specs=[pl.BlockSpec(memory_space=pltpu.SMEM)] + [anywhere] * 4,
        out_specs=(anywhere, anywhere, anywhere, pl.BlockSpec(memory_space=pltpu.VMEM)),
        scratch_shapes=[
            pltpu.VMEM((per, seq, HD), low),
            pltpu.VMEM((per, seq, HD), low),
            pltpu.VMEM((seq, HD), low),
            pltpu.VMEM((seq, HD), low),
            pltpu.VMEM((HD, seq), low),
            pltpu.VMEM((HD, seq), low),
            pltpu.VMEM((seq, TILE), wide),
            pltpu.VMEM((seq, HD), wide),
            pltpu.VMEM((seq, HD), wide),
            pltpu.VMEM((per, seq, HD), low),
            pltpu.VMEM((seq, HD), low),
            pltpu.VMEM((seq, HD), low),
            pltpu.VMEM((8, BLK), wide),
            pltpu.VMEM((dp, 8, BLK), wide),
            pltpu.SemaphoreType.DMA((per,)),
            pltpu.SemaphoreType.DMA((per,)),
            pltpu.SemaphoreType.DMA((2,)),
            pltpu.SemaphoreType.DMA((3,)),
            pltpu.SemaphoreType.DMA((7,)),
            pltpu.SemaphoreType.DMA((2,)),
        ],
        compiler_params=pltpu.CompilerParams(
            collective_id=0, has_side_effects=True, vmem_limit_bytes=62 * 1024 * 1024
        ),
        name="attention_exchange",
    )(block_mask.transpose(1, 2, 0), queries, out_grad, keys, values)
    if share > 1:
        dk = jnp.sum(dk.astype(wide), axis=0, keepdims=True).astype(low)
        dv = jnp.sum(dv.astype(wide), axis=0, keepdims=True).astype(low)
    return (dq, dk, dv, z[:per, 0])


def solution(mesh):
    return jax.shard_map(
        body,
        mesh=mesh,
        in_specs=(
            P("dp", "ctx", None),
            P("dp", "ctx", None),
            P("dp", "ctx", None),
            P("dp", "ctx", None),
            P(),
        ),
        out_specs=(P("dp", "ctx", None), P("dp", "ctx", None), P("dp", "ctx", None), P("ctx")),
        check_vma=False,
    )
```

```python
import functools
import math

import jax
import jax.numpy as jnp
from jax import lax
from jax.experimental import pallas as pl
from jax.experimental.pallas import tpu as pltpu
from jax.sharding import PartitionSpec as P

H = 32
KVH = 8
HD = 128
BLK = 128
ZLOSS = 0.05
NEG = -1e30
TILE = 2 * BLK
MESH = pl.DeviceIdType.MESH
LOG2E = math.log2(math.e)
LN2 = math.log(2.0)


def dot(a, b):
    return jnp.dot(a, b, preferred_element_type=jnp.float32)


def steps(count, step, state):
    if isinstance(count, int) and count <= 4:
        for i in range(count):
            state = step(i, state)
        return state
    return lax.fori_loop(0, count, step, state)


def rows(i, size):
    return pl.ds(i * size if isinstance(i, int) else pl.multiple_of(i * size, size), size)


def fold(x, op):
    return op(x.reshape(x.shape[0] // 8, 8, x.shape[1]), axis=0)


def kernel(
    sizes,
    mask, q_in, g_in, k_in, v_in,
    dq_out, dk_out, dv_out, z_out,
    q_all, g_all, k_all, v_all, k_tr, v_tr,
    score, dk_acc, dv_acc, dq_buf, dk_buf, dv_buf, z_own, z_all,
    q_sem, g_sem, kv_sem, out_sem, send_sem, z_sem,
):
    n, dp, per, share, tok = sizes
    seq = n * tok
    tiles = seq // TILE
    me = lax.axis_index("ctx")
    my_dp = lax.axis_index("dp")
    group = H // KVH
    scale = HD ** (-0.5)

    barrier = pltpu.get_barrier_semaphore()

    def greet(j, c):
        pl.semaphore_signal(
            barrier, inc=1, device_id=(my_dp, lax.rem(me + j, n)), device_id_type=MESH
        )
        return c

    def greet_dp(j, c):
        pl.semaphore_signal(
            barrier, inc=1, device_id=(lax.rem(my_dp + j, dp), me), device_id_type=MESH
        )
        return c

    lax.fori_loop(1, n, greet, 0)
    lax.fori_loop(1, dp, greet_dp, 0)
    pl.semaphore_wait(barrier, n - 1 + dp - 1)

    def lanes(i):
        return pl.ds(pl.multiple_of(i * HD, HD), HD)

    def remote(src, dst, send, recv, target):
        pltpu.make_async_remote_copy(
            src_ref=src, dst_ref=dst, send_sem=send, recv_sem=recv,
            device_id=(my_dp, target), device_id_type=MESH,
        ).start()

    mine = rows(me, tok)

    def kv_head(device):
        return (device * per) // group

    def send_kv(j, c):
        to = lax.rem(me + j, n)
        col = lanes(kv_head(to))
        remote(k_in.at[0, :, col], k_all.at[mine], send_sem.at[0], kv_sem.at[0], to)
        remote(v_in.at[0, :, col], v_all.at[mine], send_sem.at[1], kv_sem.at[1], to)
        return c

    lax.fori_loop(1, n, send_kv, 0)
    own = lanes(kv_head(me))
    pltpu.make_async_copy(k_in.at[0, :, own], k_all.at[mine], kv_sem.at[0]).start()
    pltpu.make_async_copy(v_in.at[0, :, own], v_all.at[mine], kv_sem.at[1]).start()

    def send_head(h, c):
        def send_q(j, c):
            to = lax.rem(me + j, n)
            col = lanes(to * per + h)
            remote(q_in.at[0, :, col], q_all.at[h, mine], send_sem.at[2], q_sem.at[h], to)
            remote(g_in.at[0, :, col], g_all.at[h, mine], send_sem.at[3], g_sem.at[h], to)
            return c

        lax.fori_loop(1, n, send_q, 0)
        col = lanes(me * per + h)
        pltpu.make_async_copy(q_in.at[0, :, col], q_all.at[h, mine], q_sem.at[h]).start()
        pltpu.make_async_copy(g_in.at[0, :, col], g_all.at[h, mine], g_sem.at[h]).start()
        return c

    lax.fori_loop(0, per, send_head, 0)

    def wait_for(ref, sem):
        pltpu.make_async_copy(ref, ref, sem).wait()

    z_own[...] = jnp.zeros_like(z_own)
    dk_acc[...] = jnp.zeros_like(dk_acc)
    dv_acc[...] = jnp.zeros_like(dv_acc)
    wait_for(k_all, kv_sem.at[0])
    wait_for(v_all, kv_sem.at[1])

    def turn(c, s):
        at = rows(c, TILE)
        k_tr[:, at] = k_all[at].astype(jnp.float32).T.astype(jnp.bfloat16)
        v_tr[:, at] = v_all[at].astype(jnp.float32).T.astype(jnp.bfloat16)
        return s

    steps(tiles, turn, 0)
    first_half = lax.broadcasted_iota(jnp.int32, (1, TILE), 1) < BLK
    causal = lax.broadcasted_iota(jnp.int32, (TILE, TILE), 0) <= lax.broadcasted_iota(
        jnp.int32, (TILE, TILE), 1
    )

    def one_head(h, c):
        wait_for(q_all.at[h], q_sem.at[h])
        wait_for(g_all.at[h], g_sem.at[h])
        head = me * per + h

        def one_tile(t):
            q_at = rows(t, TILE)
            q = q_all[h, q_at, :]
            g = g_all[h, q_at, :]
            q_tr = q.astype(jnp.float32).T.astype(jnp.bfloat16)
            g_f32 = g.astype(jnp.float32).T
            g_tr = g_f32.astype(jnp.bfloat16)

            def bias(c):
                parts = []
                for b in range(2):
                    left = mask[2 * t, 2 * c + b, head]
                    right = mask[2 * t + 1, 2 * c + b, head]
                    on = jnp.where(first_half, left, right).astype(jnp.float32)
                    parts.append(jnp.broadcast_to((1.0 - on) * NEG, (BLK, TILE)))
                return jnp.concatenate(parts, axis=0)

            def score_chunk(c, top, diagonal):
                at = rows(c, TILE)
                s = dot(k_all[at], q_tr) * (scale * LOG2E) + bias(c)
                if diagonal:
                    s = jnp.where(causal, s, NEG)
                score[at] = s
                return jnp.maximum(top, fold(s, jnp.max))

            top = jnp.full((8, TILE), NEG, jnp.float32)
            top = steps(t, lambda c, x: score_chunk(c, x, False), top)
            top = score_chunk(t, top, True)
            top = jnp.max(top, axis=0, keepdims=True)

            def exp_chunk(c, state):
                total, out = state
                at = rows(c, TILE)
                e = jnp.exp2(score[at] - top)
                score[at] = e
                out = out + dot(v_tr[:, at], e.astype(jnp.bfloat16))
                return total + fold(e, jnp.sum), out

            total, out = steps(
                t + 1, exp_chunk,
                (jnp.zeros((8, TILE), jnp.float32), jnp.zeros((HD, TILE), jnp.float32)),
            )
            total = jnp.sum(total, axis=0, keepdims=True)
            inverse = 1.0 / total
            out = (out * inverse).astype(jnp.bfloat16).astype(jnp.float32)
            delta = jnp.sum(g_f32 * out, axis=0, keepdims=True)
            log_norm = top * LN2 + jnp.log(total)
            shift = delta - (2.0 * ZLOSS) * log_norm
            square = log_norm * log_norm
            z_own[pl.ds(h, 1), :] += square[:, :BLK] + square[:, BLK:]

            def grad_chunk(c, dq):
                at = rows(c, TILE)
                p = score[at] * inverse
                dv_acc[at] += dot(p.astype(jnp.bfloat16), g)
                ds = (p * (dot(v_all[at], g_tr) - shift)).astype(jnp.bfloat16)
                dk_acc[at] += dot(ds, q)
                return dq + dot(k_tr[:, at], ds)

            dq = steps(t + 1, grad_chunk, jnp.zeros((HD, TILE), jnp.float32))
            dq_buf[h, q_at, :] = (dq * scale).T.astype(jnp.bfloat16)

            for part in range(TILE // tok):
                to = t * (TILE // tok) + part
                src = dq_buf.at[h, rows(to, tok)]
                dst = dq_out.at[0, :, lanes(head)]

                @pl.when(me == to)
                def _():
                    pltpu.make_async_copy(src, dst, out_sem.at[0]).start()

                @pl.when(me != to)
                def _():
                    remote(src, dst, send_sem.at[4], out_sem.at[0], to)

            @pl.when(h == per - 1)
            def _():
                dk_buf[q_at] = (dk_acc[q_at] * scale).astype(jnp.bfloat16)
                dv_buf[q_at] = dv_acc[q_at].astype(jnp.bfloat16)
                slot = lax.rem(me, share)
                col = lanes(kv_head(me))
                for part in range(TILE // tok):
                    to = t * (TILE // tok) + part
                    src_k = dk_buf.at[rows(to, tok)]
                    src_v = dv_buf.at[rows(to, tok)]

                    @pl.when(me == to)
                    def _():
                        pltpu.make_async_copy(src_k, dk_out.at[slot, :, col], out_sem.at[1]).start()
                        pltpu.make_async_copy(src_v, dv_out.at[slot, :, col], out_sem.at[2]).start()

                    @pl.when(me != to)
                    def _():
                        remote(src_k, dk_out.at[slot, :, col], send_sem.at[5], out_sem.at[1], to)
                        remote(src_v, dv_out.at[slot, :, col], send_sem.at[6], out_sem.at[2], to)

        if tiles <= 4:
            for t in reversed(range(tiles)):
                one_tile(t)
        else:
            def tile_step(i, s):
                one_tile(tiles - 1 - i)
                return s

            lax.fori_loop(0, tiles, tile_step, 0)
        return c

    lax.fori_loop(0, per, one_head, 0)

    pltpu.make_async_copy(z_own, z_all.at[my_dp], z_sem.at[1]).start()

    def send_z(j, c):
        pltpu.make_async_remote_copy(
            src_ref=z_own, dst_ref=z_all.at[my_dp], send_sem=z_sem.at[0], recv_sem=z_sem.at[1],
            device_id=(lax.rem(my_dp + j, dp), me), device_id_type=MESH,
        ).start()
        return c

    lax.fori_loop(1, dp, send_z, 0)
    wait_for(z_all, z_sem.at[1])
    z_sum = jnp.sum(jnp.sum(z_all[...], axis=0), axis=1, keepdims=True)
    z_out[...] = jnp.broadcast_to(z_sum * (ZLOSS / (seq * dp)), z_out.shape)

    wait_for(dq_out, out_sem.at[0])
    wait_for(dk_out, out_sem.at[1])
    wait_for(dv_out, out_sem.at[2])
    others = pl.ds(0, seq - tok)
    wide = pl.ds(0, (n - 1) * per * HD)
    wait_for(k_all.at[others], send_sem.at[0])
    wait_for(v_all.at[others], send_sem.at[1])
    wait_for(q_in.at[0, :, wide], send_sem.at[2])
    wait_for(g_in.at[0, :, wide], send_sem.at[3])
    wait_for(dq_out.at[0, :, wide], send_sem.at[4])
    wait_for(dk_buf.at[others], send_sem.at[5])
    wait_for(dv_buf.at[others], send_sem.at[6])
    wait_for(z_all.at[pl.ds(0, dp - 1)], z_sem.at[0])


def body(queries, keys, values, out_grad, block_mask):
    tok = queries.shape[1]
    n = lax.axis_size("ctx")
    dp = lax.axis_size("dp")
    per = H // n
    share = max(1, n // KVH)
    seq = tok * n
    low, wide = jnp.bfloat16, jnp.float32
    anywhere = pl.BlockSpec(memory_space=pl.ANY)
    dq, dk, dv, z = pl.pallas_call(
        functools.partial(kernel, (n, dp, per, share, tok)),
        out_shape=(
            jax.ShapeDtypeStruct(queries.shape, low),
            jax.ShapeDtypeStruct((share, tok, KVH * HD), low),
            jax.ShapeDtypeStruct((share, tok, KVH * HD), low),
            jax.ShapeDtypeStruct((8, BLK), wide),
        ),
        in_specs=[pl.BlockSpec(memory_space=pltpu.SMEM)] + [anywhere] * 4,
        out_specs=(anywhere, anywhere, anywhere, pl.BlockSpec(memory_space=pltpu.VMEM)),
        scratch_shapes=[
            pltpu.VMEM((per, seq, HD), low),
            pltpu.VMEM((per, seq, HD), low),
            pltpu.VMEM((seq, HD), low),
            pltpu.VMEM((seq, HD), low),
            pltpu.VMEM((HD, seq), low),
            pltpu.VMEM((HD, seq), low),
            pltpu.VMEM((seq, TILE), wide),
            pltpu.VMEM((seq, HD), wide),
            pltpu.VMEM((seq, HD), wide),
            pltpu.VMEM((per, seq, HD), low),
            pltpu.VMEM((seq, HD), low),
            pltpu.VMEM((seq, HD), low),
            pltpu.VMEM((8, BLK), wide),
            pltpu.VMEM((dp, 8, BLK), wide),
            pltpu.SemaphoreType.DMA((per,)),
            pltpu.SemaphoreType.DMA((per,)),
            pltpu.SemaphoreType.DMA((2,)),
            pltpu.SemaphoreType.DMA((3,)),
            pltpu.SemaphoreType.DMA((7,)),
            pltpu.SemaphoreType.DMA((2,)),
        ],
        compiler_params=pltpu.CompilerParams(
            collective_id=0, has_side_effects=True, vmem_limit_bytes=62 * 1024 * 1024
        ),
        name="attention_exchange",
    )(block_mask.transpose(1, 2, 0), queries, out_grad, keys, values)
    if share > 1:
        dk = jnp.sum(dk.astype(wide), axis=0, keepdims=True).astype(low)
        dv = jnp.sum(dv.astype(wide), axis=0, keepdims=True).astype(low)
    return (dq, dk, dv, z[:per, 0])


def quad_kernel(
    dp,
    mask, q_in, g_in, k_in, v_in,
    dq_out, dk_out, dv_out, z_out,
    q_all, g_all, k_all, v_all, k_tr, v_tr,
    score, dk_acc, dv_acc, dq_buf, dk_buf, dv_buf, dk_part, dv_part, z_own, z_set, z_all,
    q_sem, g_sem, k_sem, v_sem, dq_sem, dk_sem, dv_sem, send_sem, z_sem,
):
    n, tok, per = 8, BLK, H // KVH
    seq = n * tok
    me = lax.axis_index("ctx")
    my_dp = lax.axis_index("dp")
    y, x, core = me // 4, lax.rem(me // 2, 2), lax.rem(me, 2)
    chip = me // 2
    scale = HD ** (-0.5)

    barrier = pltpu.get_barrier_semaphore()

    def greet(j, c):
        pl.semaphore_signal(
            barrier, inc=1, device_id=(my_dp, lax.rem(me + j, n)), device_id_type=MESH
        )
        return c

    def greet_dp(j, c):
        pl.semaphore_signal(
            barrier, inc=1, device_id=(lax.rem(my_dp + j, dp), me), device_id_type=MESH
        )
        return c

    lax.fori_loop(1, n, greet, 0)
    lax.fori_loop(1, dp, greet_dp, 0)
    pl.semaphore_wait(barrier, n - 1 + dp - 1)

    def lanes(i):
        return pl.ds(pl.multiple_of(i * HD, HD), HD)

    def remote(src, dst, send, recv, target):
        pltpu.make_async_remote_copy(
            src_ref=src, dst_ref=dst, send_sem=send, recv_sem=recv,
            device_id=(my_dp, target), device_id_type=MESH,
        ).start()

    def move(src, dst, send, recv, target):
        @pl.when(target == me)
        def _():
            pltpu.make_async_copy(src, dst, recv).start()

        @pl.when(target != me)
        def _():
            remote(src, dst, send, recv, target)

    def wait_for(ref, sem):
        pltpu.make_async_copy(ref, ref, sem).wait()

    def kv_head(group, to):
        first = 2 * lax.rem(to // 2, 2) + lax.rem(to, 2)
        second = 4 + 2 * (to // 4) + lax.rem(to, 2)
        return first if group == 0 else second

    mine = rows(me, tok)

    def send_kv(group):
        def one(j, c):
            to = lax.rem(me + j, n)
            last = 2 * (to // 4) + 1 if group == 0 else 2 + lax.rem(to // 2, 2)

            @pl.when(chip <= last)
            def _():
                col = lanes(kv_head(group, to))
                move(k_in.at[0, :, col], k_all.at[group, mine], send_sem.at[group],
                     k_sem.at[group * 4 + chip], to)
                move(v_in.at[0, :, col], v_all.at[group, mine], send_sem.at[2 + group],
                     v_sem.at[group * 4 + chip], to)

            return c

        lax.fori_loop(0, n, one, 0)

    def send_q(group, m):
        item = 2 * m + group
        slot = x if group == 0 else y
        place = rows(2 * slot + core, tok)

        def one(j, c):
            far = lax.rem((x if group == 0 else y) + j // 2, 2)
            to = 2 * far + lax.rem(core + j, 2) + (4 * y if group == 0 else 0)
            if group == 1:
                to = 4 * far + 2 * x + lax.rem(core + j, 2)
            col = lanes(kv_head(group, to) * per + m)
            at = item * 2 + slot
            move(q_in.at[0, :, col], q_all.at[item, place], send_sem.at[4], q_sem.at[at], to)
            move(g_in.at[0, :, col], g_all.at[item, place], send_sem.at[5], g_sem.at[at], to)
            return c

        lax.fori_loop(0, 4, one, 0)

    def send_pair(m, c):
        send_q(0, m)
        send_q(1, m)
        return c

    send_kv(0)
    send_q(0, 0)
    send_kv(1)
    send_q(1, 0)
    lax.fori_loop(1, per, send_pair, 0)

    z_own[...] = jnp.zeros_like(z_own)
    dk_acc[...] = jnp.zeros_like(dk_acc)
    dv_acc[...] = jnp.zeros_like(dv_acc)
    first_half = lax.broadcasted_iota(jnp.int32, (1, TILE), 1) < BLK
    causal = lax.broadcasted_iota(jnp.int32, (TILE, TILE), 0) <= lax.broadcasted_iota(
        jnp.int32, (TILE, TILE), 1
    )

    def prepare(group, last):
        def one(c, carry):
            at = rows(c, TILE)
            wait_for(k_all.at[group, at], k_sem.at[group * 4 + c])
            wait_for(v_all.at[group, at], v_sem.at[group * 4 + c])
            k_tr[group, :, at] = k_all[group, at, :].astype(jnp.float32).T.astype(jnp.bfloat16)
            v_tr[group, :, at] = v_all[group, at, :].astype(jnp.float32).T.astype(jnp.bfloat16)
            return carry

        lax.fori_loop(0, last + 1, one, 0)

    def one_tile(t, group, head, item, slot):
        q_at = rows(slot, TILE)
        q = q_all[item, q_at, :]
        g = g_all[item, q_at, :]
        q_tr = q.astype(jnp.float32).T.astype(jnp.bfloat16)
        g_f32 = g.astype(jnp.float32).T
        g_tr = g_f32.astype(jnp.bfloat16)

        def bias(c):
            parts = []
            for b in range(2):
                left = mask[2 * t, 2 * c + b, head]
                right = mask[2 * t + 1, 2 * c + b, head]
                on = jnp.where(first_half, left, right).astype(jnp.float32)
                parts.append(jnp.broadcast_to((1.0 - on) * NEG, (BLK, TILE)))
            return jnp.concatenate(parts, axis=0)

        top = jnp.full((8, TILE), NEG, jnp.float32)
        for c in range(t + 1):
            at = rows(c, TILE)
            s = dot(k_all[group, at, :], q_tr) * (scale * LOG2E) + bias(c)
            if c == t:
                s = jnp.where(causal, s, NEG)
            score[at] = s
            top = jnp.maximum(top, fold(s, jnp.max))
        top = jnp.max(top, axis=0, keepdims=True)

        total = jnp.zeros((8, TILE), jnp.float32)
        out = jnp.zeros((HD, TILE), jnp.float32)
        for c in range(t + 1):
            at = rows(c, TILE)
            e = jnp.exp2(score[at] - top)
            score[at] = e
            out = out + dot(v_tr[group, :, at], e.astype(jnp.bfloat16))
            total = total + fold(e, jnp.sum)
        total = jnp.sum(total, axis=0, keepdims=True)
        inverse = 1.0 / total
        out = (out * inverse).astype(jnp.bfloat16).astype(jnp.float32)
        delta = jnp.sum(g_f32 * out, axis=0, keepdims=True)
        log_norm = top * LN2 + jnp.log(total)
        shift = delta - (2.0 * ZLOSS) * log_norm
        square = log_norm * log_norm
        z_own[group, pl.ds(lax.rem(head, per), 1), :] += square[:, :BLK] + square[:, BLK:]

        dq = jnp.zeros((HD, TILE), jnp.float32)
        for c in range(t + 1):
            at = rows(c, TILE)
            p = score[at] * inverse
            dv_acc[group, at, :] += dot(p.astype(jnp.bfloat16), g)
            ds = (p * (dot(v_all[group, at, :], g_tr) - shift)).astype(jnp.bfloat16)
            dk_acc[group, at, :] += dot(ds, q)
            dq = dq + dot(k_tr[group, :, at], ds)
        dq_buf[item, q_at, :] = (dq * scale).T.astype(jnp.bfloat16)

    def one_step(step, carry):
        item = step // 2
        slot = 1 - lax.rem(step, 2)
        group = lax.rem(item, 2)
        m = item // 2
        is_first = group == 0
        head_kv = jnp.where(is_first, kv_head(0, me), kv_head(1, me))
        head = head_kv * per + m
        low = jnp.where(is_first, 2 * y, x)
        high = jnp.where(is_first, 2 * y + 1, 2 + x)
        tile = jnp.where(slot == 1, high, low)

        @pl.when((m == 0) & (slot == 1))
        def _():
            prepare(group, high)

        at = item * 2 + slot
        wait_for(q_all.at[item, rows(slot, TILE)], q_sem.at[at])
        wait_for(g_all.at[item, rows(slot, TILE)], g_sem.at[at])
        for t in range(4):
            @pl.when(tile == t)
            def _(t=t):
                one_tile(t, group, head, item, slot)

        def give_dq(part, c):
            move(dq_buf.at[item, rows(2 * slot + part, tok)], dq_out.at[0, :, lanes(head)],
                 send_sem.at[6], dq_sem.at[0], 2 * tile + part)
            return c

        lax.fori_loop(0, 2, give_dq, 0)

        @pl.when(m == per - 1)
        def _():
            token_set = jnp.where(is_first, y, x)
            sem = group * 2 + token_set
            col = lanes(head_kv)

            def give(c, carry):
                keys_at = rows(c, TILE)
                dk_buf[group, keys_at, :] = (dk_acc[group, keys_at, :] * scale).astype(jnp.bfloat16)
                dv_buf[group, keys_at, :] = dv_acc[group, keys_at, :].astype(jnp.bfloat16)
                for part in range(2):
                    to = 2 * c + part
                    move(dk_buf.at[group, rows(to, tok)], dk_part.at[token_set, :, col],
                         send_sem.at[7 + group], dk_sem.at[sem], to)
                    move(dv_buf.at[group, rows(to, tok)], dv_part.at[token_set, :, col],
                         send_sem.at[9 + group], dv_sem.at[sem], to)
                return carry

            lax.fori_loop(jnp.where(slot == 1, low + 1, 0), tile + 1, give, 0)

        return carry

    lax.fori_loop(0, 4 * per, one_step, 0)

    move(z_own.at[0], z_set.at[y], z_sem.at[0], z_sem.at[2 + y], kv_head(0, me))
    move(z_own.at[1], z_set.at[x], z_sem.at[1], z_sem.at[2 + x], kv_head(1, me))
    wait_for(z_set.at[0], z_sem.at[2])
    wait_for(z_set.at[1], z_sem.at[3])
    z_all[my_dp] = z_set[0] + z_set[1]

    def send_z(j, c):
        pltpu.make_async_remote_copy(
            src_ref=z_all.at[my_dp], dst_ref=z_all.at[my_dp],
            send_sem=z_sem.at[4], recv_sem=z_sem.at[5],
            device_id=(lax.rem(my_dp + j, dp), me), device_id_type=MESH,
        ).start()
        return c

    lax.fori_loop(1, dp, send_z, 0)
    wait_for(z_all.at[pl.ds(0, dp - 1)], z_sem.at[5])
    z_sum = jnp.sum(jnp.sum(z_all[...], axis=0), axis=1, keepdims=True)
    z_out[...] = jnp.broadcast_to(z_sum * (ZLOSS / (seq * dp)), z_out.shape)

    for group in range(2):
        cols = pl.ds(group * 4 * HD, 4 * HD)
        both = (y == 0) if group == 0 else (chip < 3)
        for part, sems, result in ((dk_part, dk_sem, dk_out), (dv_part, dv_sem, dv_out)):
            wait_for(part.at[1, :, cols], sems.at[group * 2 + 1])

            @pl.when(both)
            def _(part=part, sems=sems, result=result):
                wait_for(part.at[0, :, cols], sems.at[group * 2])
                result[0, :, cols] = (
                    part[0, :, cols].astype(jnp.float32) + part[1, :, cols].astype(jnp.float32)
                ).astype(jnp.bfloat16)

            @pl.when(jnp.logical_not(both))
            def _(part=part, result=result):
                result[0, :, cols] = part[1, :, cols]

    wait_for(dq_out, dq_sem.at[0])

    def sent(ref, sem, count):
        wait_for(ref.at[pl.ds(0, count * tok)], sem)

    for group in range(2):
        late = (y == 1) if group == 0 else (chip == 3)
        for sem in (group, 2 + group):
            @pl.when(late)
            def _(sem=sem):
                sent(k_all.at[0], send_sem.at[sem], 3)

            @pl.when(jnp.logical_not(late))
            def _(sem=sem):
                sent(k_all.at[0], send_sem.at[sem], 7)

        whole = (y == 1) if group == 0 else (x == 1)
        for sem in (7 + group, 9 + group):
            @pl.when(whole)
            def _(sem=sem):
                sent(k_all.at[0], send_sem.at[sem], 7)

            @pl.when(jnp.logical_not(whole))
            def _(sem=sem):
                sent(k_all.at[0], send_sem.at[sem], 3 if group == 0 else 5)

        @pl.when(kv_head(group, me) != me)
        def _():
            wait_for(z_own.at[group], z_sem.at[group])

    wide = pl.ds(0, 24 * HD)
    for sem in (4, 5, 6):
        wait_for(dq_out.at[0, :, wide], send_sem.at[sem])
    wait_for(z_all.at[pl.ds(0, dp - 1)], z_sem.at[4])


def finish_kernel(dq, dk, dv, z, dq_out, dk_out, dv_out, z_out, sem):
    copies = []
    for a, b, parts in ((dq, dq_out, 8), (dk, dk_out, 2), (dv, dv_out, 2)):
        size = a.shape[1] // parts
        for i in range(parts):
            part = pl.ds(i * size, size)
            copies.append(
                pltpu.make_async_copy(a.at[:, part], b.at[:, part], sem.at[len(copies)])
            )
    for copy in copies:
        copy.start()
    for h in range(z_out.shape[0]):
        z_out[h] = z[h, 0]
    for copy in copies:
        copy.wait()


def quad_body(queries, keys, values, out_grad, block_mask):
    dp = lax.axis_size("dp")
    seq, items = 8 * BLK, 8
    low, wide = jnp.bfloat16, jnp.float32
    hbm = pl.BlockSpec(memory_space=pltpu.HBM)
    vmem = pl.BlockSpec(memory_space=pltpu.VMEM)
    smem = pl.BlockSpec(memory_space=pltpu.SMEM)
    shape = jax.ShapeDtypeStruct
    results = pl.pallas_call(
        functools.partial(quad_kernel, dp),
        out_shape=(
            shape(queries.shape, low), shape(keys.shape, low), shape(keys.shape, low),
            shape((8, BLK), wide),
        ),
        in_specs=[smem] + [hbm] * 4,
        out_specs=(hbm, vmem, vmem, vmem),
        scratch_shapes=[
            pltpu.VMEM((items, 2 * TILE, HD), low),
            pltpu.VMEM((items, 2 * TILE, HD), low),
            pltpu.VMEM((2, seq, HD), low),
            pltpu.VMEM((2, seq, HD), low),
            pltpu.VMEM((2, HD, seq), low),
            pltpu.VMEM((2, HD, seq), low),
            pltpu.VMEM((seq, TILE), wide),
            pltpu.VMEM((2, seq, HD), wide),
            pltpu.VMEM((2, seq, HD), wide),
            pltpu.VMEM((items, 2 * TILE, HD), low),
            pltpu.VMEM((2, seq, HD), low),
            pltpu.VMEM((2, seq, HD), low),
            pltpu.VMEM((2, BLK, KVH * HD), low),
            pltpu.VMEM((2, BLK, KVH * HD), low),
            pltpu.VMEM((2, 8, BLK), wide),
            pltpu.VMEM((2, 8, BLK), wide),
            pltpu.VMEM((dp, 8, BLK), wide),
            pltpu.SemaphoreType.DMA((2 * items,)),
            pltpu.SemaphoreType.DMA((2 * items,)),
            pltpu.SemaphoreType.DMA((8,)),
            pltpu.SemaphoreType.DMA((8,)),
            pltpu.SemaphoreType.DMA((1,)),
            pltpu.SemaphoreType.DMA((4,)),
            pltpu.SemaphoreType.DMA((4,)),
            pltpu.SemaphoreType.DMA((11,)),
            pltpu.SemaphoreType.DMA((6,)),
        ],
        compiler_params=pltpu.CompilerParams(
            collective_id=0, has_side_effects=True, vmem_limit_bytes=60 * 1024 * 1024
        ),
        name="attention_exchange",
    )(block_mask.transpose(1, 2, 0), queries, out_grad, keys, values)
    return pl.pallas_call(
        finish_kernel,
        out_shape=(
            shape(queries.shape, low), shape(keys.shape, low), shape(keys.shape, low),
            shape((H // 8,), wide),
        ),
        in_specs=[hbm, hbm, hbm, smem],
        out_specs=(hbm, hbm, hbm, smem),
        scratch_shapes=[pltpu.SemaphoreType.DMA((12,))],
        compiler_params=pltpu.CompilerParams(vmem_limit_bytes=62 * 1024 * 1024),
        name="write_results",
    )(*results)


def solution(mesh):
    quad = mesh.shape["ctx"] == 8
    return jax.shard_map(
        quad_body if quad else body,
        mesh=mesh,
        in_specs=(
            P("dp", "ctx", None),
            P("dp", "ctx", None),
            P("dp", "ctx", None),
            P("dp", "ctx", None),
            P(),
        ),
        out_specs=(P("dp", "ctx", None), P("dp", "ctx", None), P("dp", "ctx", None), P("ctx")),
        check_vma=False,
    )
```

```python
import functools
import math

import jax
import jax.numpy as jnp
from jax import lax
from jax.experimental import pallas as pl
from jax.experimental.pallas import tpu as pltpu
from jax.sharding import PartitionSpec as P

H = 32
KVH = 8
HD = 128
BLK = 128
ZLOSS = 0.05
NEG = -1e30
TILE = 2 * BLK
MESH = pl.DeviceIdType.MESH
LOG2E = math.log2(math.e)
LN2 = math.log(2.0)


def dot(a, b):
    return jnp.dot(a, b, preferred_element_type=jnp.float32)


def steps(count, step, state):
    if isinstance(count, int) and count <= 4:
        for i in range(count):
            state = step(i, state)
        return state
    return lax.fori_loop(0, count, step, state)


def rows(i, size):
    return pl.ds(i * size if isinstance(i, int) else pl.multiple_of(i * size, size), size)


def fold(x, op):
    return op(x.reshape(x.shape[0] // 8, 8, x.shape[1]), axis=0)


def kernel(
    sizes,
    mask, q_in, g_in, k_in, v_in,
    dq_out, dk_out, dv_out, z_out,
    q_all, g_all, k_all, v_all, k_tr, v_tr,
    score, dk_acc, dv_acc, dq_buf, dk_buf, dv_buf, z_own, z_all,
    q_sem, g_sem, kv_sem, out_sem, send_sem, z_sem,
):
    n, dp, per, share, tok = sizes
    seq = n * tok
    tiles = seq // TILE
    me = lax.axis_index("ctx")
    my_dp = lax.axis_index("dp")
    group = H // KVH
    scale = HD ** (-0.5)

    barrier = pltpu.get_barrier_semaphore()

    def greet(j, c):
        pl.semaphore_signal(
            barrier, inc=1, device_id=(my_dp, lax.rem(me + j, n)), device_id_type=MESH
        )
        return c

    def greet_dp(j, c):
        pl.semaphore_signal(
            barrier, inc=1, device_id=(lax.rem(my_dp + j, dp), me), device_id_type=MESH
        )
        return c

    lax.fori_loop(1, n, greet, 0)
    lax.fori_loop(1, dp, greet_dp, 0)
    pl.semaphore_wait(barrier, n - 1 + dp - 1)

    def lanes(i):
        return pl.ds(pl.multiple_of(i * HD, HD), HD)

    def remote(src, dst, send, recv, target):
        pltpu.make_async_remote_copy(
            src_ref=src, dst_ref=dst, send_sem=send, recv_sem=recv,
            device_id=(my_dp, target), device_id_type=MESH,
        ).start()

    mine = rows(me, tok)

    def kv_head(device):
        return (device * per) // group

    def send_kv(j, c):
        to = lax.rem(me + j, n)
        col = lanes(kv_head(to))
        remote(k_in.at[0, :, col], k_all.at[mine], send_sem.at[0], kv_sem.at[0], to)
        remote(v_in.at[0, :, col], v_all.at[mine], send_sem.at[1], kv_sem.at[1], to)
        return c

    lax.fori_loop(1, n, send_kv, 0)
    own = lanes(kv_head(me))
    pltpu.make_async_copy(k_in.at[0, :, own], k_all.at[mine], kv_sem.at[0]).start()
    pltpu.make_async_copy(v_in.at[0, :, own], v_all.at[mine], kv_sem.at[1]).start()

    def send_head(h, c):
        def send_q(j, c):
            to = lax.rem(me + j, n)
            col = lanes(to * per + h)
            remote(q_in.at[0, :, col], q_all.at[h, mine], send_sem.at[2], q_sem.at[h], to)
            remote(g_in.at[0, :, col], g_all.at[h, mine], send_sem.at[3], g_sem.at[h], to)
            return c

        lax.fori_loop(1, n, send_q, 0)
        col = lanes(me * per + h)
        pltpu.make_async_copy(q_in.at[0, :, col], q_all.at[h, mine], q_sem.at[h]).start()
        pltpu.make_async_copy(g_in.at[0, :, col], g_all.at[h, mine], g_sem.at[h]).start()
        return c

    lax.fori_loop(0, per, send_head, 0)

    def wait_for(ref, sem):
        pltpu.make_async_copy(ref, ref, sem).wait()

    z_own[...] = jnp.zeros_like(z_own)
    dk_acc[...] = jnp.zeros_like(dk_acc)
    dv_acc[...] = jnp.zeros_like(dv_acc)
    wait_for(k_all, kv_sem.at[0])
    wait_for(v_all, kv_sem.at[1])

    def turn(c, s):
        at = rows(c, TILE)
        k_tr[:, at] = k_all[at].astype(jnp.float32).T.astype(jnp.bfloat16)
        v_tr[:, at] = v_all[at].astype(jnp.float32).T.astype(jnp.bfloat16)
        return s

    steps(tiles, turn, 0)
    first_half = lax.broadcasted_iota(jnp.int32, (1, TILE), 1) < BLK
    causal = lax.broadcasted_iota(jnp.int32, (TILE, TILE), 0) <= lax.broadcasted_iota(
        jnp.int32, (TILE, TILE), 1
    )

    def one_head(h, c):
        wait_for(q_all.at[h], q_sem.at[h])
        wait_for(g_all.at[h], g_sem.at[h])
        head = me * per + h

        def one_tile(t):
            q_at = rows(t, TILE)
            q = q_all[h, q_at, :]
            g = g_all[h, q_at, :]
            q_tr = q.astype(jnp.float32).T.astype(jnp.bfloat16)
            g_f32 = g.astype(jnp.float32).T
            g_tr = g_f32.astype(jnp.bfloat16)

            def bias(c):
                parts = []
                for b in range(2):
                    left = mask[2 * t, 2 * c + b, head]
                    right = mask[2 * t + 1, 2 * c + b, head]
                    on = jnp.where(first_half, left, right).astype(jnp.float32)
                    parts.append(jnp.broadcast_to((1.0 - on) * NEG, (BLK, TILE)))
                return jnp.concatenate(parts, axis=0)

            def score_chunk(c, top, diagonal):
                at = rows(c, TILE)
                s = dot(k_all[at], q_tr) * (scale * LOG2E) + bias(c)
                if diagonal:
                    s = jnp.where(causal, s, NEG)
                score[at] = s
                return jnp.maximum(top, fold(s, jnp.max))

            top = jnp.full((8, TILE), NEG, jnp.float32)
            top = steps(t, lambda c, x: score_chunk(c, x, False), top)
            top = score_chunk(t, top, True)
            top = jnp.max(top, axis=0, keepdims=True)

            def exp_chunk(c, state):
                total, out = state
                at = rows(c, TILE)
                e = jnp.exp2(score[at] - top)
                score[at] = e
                out = out + dot(v_tr[:, at], e.astype(jnp.bfloat16))
                return total + fold(e, jnp.sum), out

            total, out = steps(
                t + 1, exp_chunk,
                (jnp.zeros((8, TILE), jnp.float32), jnp.zeros((HD, TILE), jnp.float32)),
            )
            total = jnp.sum(total, axis=0, keepdims=True)
            inverse = 1.0 / total
            out = (out * inverse).astype(jnp.bfloat16).astype(jnp.float32)
            delta = jnp.sum(g_f32 * out, axis=0, keepdims=True)
            log_norm = top * LN2 + jnp.log(total)
            shift = delta - (2.0 * ZLOSS) * log_norm
            square = log_norm * log_norm
            z_own[pl.ds(h, 1), :] += square[:, :BLK] + square[:, BLK:]

            def grad_chunk(c, dq):
                at = rows(c, TILE)
                p = score[at] * inverse
                dv_acc[at] += dot(p.astype(jnp.bfloat16), g)
                ds = (p * (dot(v_all[at], g_tr) - shift)).astype(jnp.bfloat16)
                dk_acc[at] += dot(ds, q)
                return dq + dot(k_tr[:, at], ds)

            dq = steps(t + 1, grad_chunk, jnp.zeros((HD, TILE), jnp.float32))
            dq_buf[h, q_at, :] = (dq * scale).T.astype(jnp.bfloat16)

            for part in range(TILE // tok):
                to = t * (TILE // tok) + part
                src = dq_buf.at[h, rows(to, tok)]
                dst = dq_out.at[0, :, lanes(head)]

                @pl.when(me == to)
                def _():
                    pltpu.make_async_copy(src, dst, out_sem.at[0]).start()

                @pl.when(me != to)
                def _():
                    remote(src, dst, send_sem.at[4], out_sem.at[0], to)

            @pl.when(h == per - 1)
            def _():
                dk_buf[q_at] = (dk_acc[q_at] * scale).astype(jnp.bfloat16)
                dv_buf[q_at] = dv_acc[q_at].astype(jnp.bfloat16)
                slot = lax.rem(me, share)
                col = lanes(kv_head(me))
                for part in range(TILE // tok):
                    to = t * (TILE // tok) + part
                    src_k = dk_buf.at[rows(to, tok)]
                    src_v = dv_buf.at[rows(to, tok)]

                    @pl.when(me == to)
                    def _():
                        pltpu.make_async_copy(src_k, dk_out.at[slot, :, col], out_sem.at[1]).start()
                        pltpu.make_async_copy(src_v, dv_out.at[slot, :, col], out_sem.at[2]).start()

                    @pl.when(me != to)
                    def _():
                        remote(src_k, dk_out.at[slot, :, col], send_sem.at[5], out_sem.at[1], to)
                        remote(src_v, dv_out.at[slot, :, col], send_sem.at[6], out_sem.at[2], to)

        if tiles <= 4:
            for t in reversed(range(tiles)):
                one_tile(t)
        else:
            def tile_step(i, s):
                one_tile(tiles - 1 - i)
                return s

            lax.fori_loop(0, tiles, tile_step, 0)
        return c

    lax.fori_loop(0, per, one_head, 0)

    pltpu.make_async_copy(z_own, z_all.at[my_dp], z_sem.at[1]).start()

    def send_z(j, c):
        pltpu.make_async_remote_copy(
            src_ref=z_own, dst_ref=z_all.at[my_dp], send_sem=z_sem.at[0], recv_sem=z_sem.at[1],
            device_id=(lax.rem(my_dp + j, dp), me), device_id_type=MESH,
        ).start()
        return c

    lax.fori_loop(1, dp, send_z, 0)
    wait_for(z_all, z_sem.at[1])
    z_sum = jnp.sum(jnp.sum(z_all[...], axis=0), axis=1, keepdims=True)
    z_out[...] = jnp.broadcast_to(z_sum * (ZLOSS / (seq * dp)), z_out.shape)

    wait_for(dq_out, out_sem.at[0])
    wait_for(dk_out, out_sem.at[1])
    wait_for(dv_out, out_sem.at[2])
    others = pl.ds(0, seq - tok)
    wide = pl.ds(0, (n - 1) * per * HD)
    wait_for(k_all.at[others], send_sem.at[0])
    wait_for(v_all.at[others], send_sem.at[1])
    wait_for(q_in.at[0, :, wide], send_sem.at[2])
    wait_for(g_in.at[0, :, wide], send_sem.at[3])
    wait_for(dq_out.at[0, :, wide], send_sem.at[4])
    wait_for(dk_buf.at[others], send_sem.at[5])
    wait_for(dv_buf.at[others], send_sem.at[6])
    wait_for(z_all.at[pl.ds(0, dp - 1)], z_sem.at[0])


def body(queries, keys, values, out_grad, block_mask):
    tok = queries.shape[1]
    n = lax.axis_size("ctx")
    dp = lax.axis_size("dp")
    per = H // n
    share = max(1, n // KVH)
    seq = tok * n
    low, wide = jnp.bfloat16, jnp.float32
    anywhere = pl.BlockSpec(memory_space=pl.ANY)
    dq, dk, dv, z = pl.pallas_call(
        functools.partial(kernel, (n, dp, per, share, tok)),
        out_shape=(
            jax.ShapeDtypeStruct(queries.shape, low),
            jax.ShapeDtypeStruct((share, tok, KVH * HD), low),
            jax.ShapeDtypeStruct((share, tok, KVH * HD), low),
            jax.ShapeDtypeStruct((8, BLK), wide),
        ),
        in_specs=[pl.BlockSpec(memory_space=pltpu.SMEM)] + [anywhere] * 4,
        out_specs=(anywhere, anywhere, anywhere, pl.BlockSpec(memory_space=pltpu.VMEM)),
        scratch_shapes=[
            pltpu.VMEM((per, seq, HD), low),
            pltpu.VMEM((per, seq, HD), low),
            pltpu.VMEM((seq, HD), low),
            pltpu.VMEM((seq, HD), low),
            pltpu.VMEM((HD, seq), low),
            pltpu.VMEM((HD, seq), low),
            pltpu.VMEM((seq, TILE), wide),
            pltpu.VMEM((seq, HD), wide),
            pltpu.VMEM((seq, HD), wide),
            pltpu.VMEM((per, seq, HD), low),
            pltpu.VMEM((seq, HD), low),
            pltpu.VMEM((seq, HD), low),
            pltpu.VMEM((8, BLK), wide),
            pltpu.VMEM((dp, 8, BLK), wide),
            pltpu.SemaphoreType.DMA((per,)),
            pltpu.SemaphoreType.DMA((per,)),
            pltpu.SemaphoreType.DMA((2,)),
            pltpu.SemaphoreType.DMA((3,)),
            pltpu.SemaphoreType.DMA((7,)),
            pltpu.SemaphoreType.DMA((2,)),
        ],
        compiler_params=pltpu.CompilerParams(
            collective_id=0, has_side_effects=True, vmem_limit_bytes=62 * 1024 * 1024
        ),
        name="attention_exchange",
    )(block_mask.transpose(1, 2, 0), queries, out_grad, keys, values)
    if share > 1:
        dk = jnp.sum(dk.astype(wide), axis=0, keepdims=True).astype(low)
        dv = jnp.sum(dv.astype(wide), axis=0, keepdims=True).astype(low)
    return (dq, dk, dv, z[:per, 0])


def quad_kernel(
    dp,
    mask, q_in, g_in, k_in, v_in,
    dq_out, dk_out, dv_out, z_out,
    q_all, g_all, k_all, v_all, k_tr, v_tr,
    score, p_low, ds_low, dk_acc, dv_acc, dq_buf, dk_buf, dv_buf, dk_part, dv_part, z_own, z_set, z_all,
    q_sem, g_sem, k_sem, v_sem, dq_sem, dk_sem, dv_sem, send_sem, z_sem,
):
    n, tok, per = 8, BLK, H // KVH
    seq = n * tok
    me = lax.axis_index("ctx")
    my_dp = lax.axis_index("dp")
    y, x, core = me // 4, lax.rem(me // 2, 2), lax.rem(me, 2)
    chip = me // 2
    scale = HD ** (-0.5)

    barrier = pltpu.get_barrier_semaphore()

    def greet(j, c):
        pl.semaphore_signal(
            barrier, inc=1, device_id=(my_dp, lax.rem(me + j, n)), device_id_type=MESH
        )
        return c

    def greet_dp(j, c):
        pl.semaphore_signal(
            barrier, inc=1, device_id=(lax.rem(my_dp + j, dp), me), device_id_type=MESH
        )
        return c

    lax.fori_loop(1, n, greet, 0)
    lax.fori_loop(1, dp, greet_dp, 0)
    pl.semaphore_wait(barrier, n - 1 + dp - 1)

    def lanes(i):
        return pl.ds(pl.multiple_of(i * HD, HD), HD)

    def remote(src, dst, send, recv, target):
        pltpu.make_async_remote_copy(
            src_ref=src, dst_ref=dst, send_sem=send, recv_sem=recv,
            device_id=(my_dp, target), device_id_type=MESH,
        ).start()

    def move(src, dst, send, recv, target):
        @pl.when(target == me)
        def _():
            pltpu.make_async_copy(src, dst, recv).start()

        @pl.when(target != me)
        def _():
            remote(src, dst, send, recv, target)

    def wait_for(ref, sem):
        pltpu.make_async_copy(ref, ref, sem).wait()

    def kv_head(group, to):
        first = 2 * lax.rem(to // 2, 2) + lax.rem(to, 2)
        second = 4 + 2 * (to // 4) + lax.rem(to, 2)
        return first if group == 0 else second

    mine = rows(me, tok)

    def send_kv(group):
        def one(j, c):
            to = lax.rem(me + j, n)
            last = 2 * (to // 4) + 1 if group == 0 else 2 + lax.rem(to // 2, 2)

            @pl.when(chip <= last)
            def _():
                col = lanes(kv_head(group, to))
                move(k_in.at[0, :, col], k_all.at[group, mine], send_sem.at[group],
                     k_sem.at[group * 4 + chip], to)
                move(v_in.at[0, :, col], v_all.at[group, mine], send_sem.at[2 + group],
                     v_sem.at[group * 4 + chip], to)

            return c

        lax.fori_loop(0, n, one, 0)

    def send_q(group, m):
        item = 2 * m + group
        slot = x if group == 0 else y
        place = rows(2 * slot + core, tok)

        def one(j, c):
            far = lax.rem((x if group == 0 else y) + j // 2, 2)
            to = 2 * far + lax.rem(core + j, 2) + (4 * y if group == 0 else 0)
            if group == 1:
                to = 4 * far + 2 * x + lax.rem(core + j, 2)
            col = lanes(kv_head(group, to) * per + m)
            at = item * 2 + slot
            move(q_in.at[0, :, col], q_all.at[item, place], send_sem.at[4], q_sem.at[at], to)
            move(g_in.at[0, :, col], g_all.at[item, place], send_sem.at[5], g_sem.at[at], to)
            return c

        lax.fori_loop(0, 4, one, 0)

    def send_pair(m, c):
        send_q(0, m)
        send_q(1, m)
        return c

    send_kv(0)
    send_q(0, 0)
    send_kv(1)
    send_q(1, 0)
    lax.fori_loop(1, per, send_pair, 0)

    z_own[...] = jnp.zeros_like(z_own)
    dk_acc[...] = jnp.zeros_like(dk_acc)
    dv_acc[...] = jnp.zeros_like(dv_acc)
    first_half = lax.broadcasted_iota(jnp.int32, (1, TILE), 1) < BLK
    causal = lax.broadcasted_iota(jnp.int32, (TILE, TILE), 0) <= lax.broadcasted_iota(
        jnp.int32, (TILE, TILE), 1
    )

    def prepare(group, last):
        def one(c, carry):
            at = rows(c, TILE)
            wait_for(k_all.at[group, at], k_sem.at[group * 4 + c])
            wait_for(v_all.at[group, at], v_sem.at[group * 4 + c])
            k_tr[group, :, at] = k_all[group, at, :].astype(jnp.float32).T.astype(jnp.bfloat16)
            v_tr[group, :, at] = v_all[group, at, :].astype(jnp.float32).T.astype(jnp.bfloat16)
            return carry

        lax.fori_loop(0, last + 1, one, 0)

    def tile_pair(pair, group, head, item):
        work = []
        for slot, t in ((1, pair[1]), (0, pair[0])):
            q = q_all[item, rows(slot, TILE), :]
            g = g_all[item, rows(slot, TILE), :]
            g_f32 = g.astype(jnp.float32).T
            work.append(dict(
                slot=slot, t=t, span=pl.ds(0, (t + 1) * TILE), q=q, g=g, g_f32=g_f32,
                q_tr=q.astype(jnp.float32).T.astype(jnp.bfloat16), g_tr=g_f32.astype(jnp.bfloat16),
            ))

        def bias(t, c):
            parts = []
            for b in range(2):
                left = mask[2 * t, 2 * c + b, head]
                right = mask[2 * t + 1, 2 * c + b, head]
                on = jnp.where(first_half, left, right).astype(jnp.float32)
                parts.append(jnp.broadcast_to((1.0 - on) * NEG, (BLK, TILE)))
            return jnp.concatenate(parts, axis=0)

        for w in work:
            w["raw"] = dot(k_all[group, w["span"], :], w["q_tr"])
        for w in work:
            t, slot = w["t"], w["slot"]
            top = jnp.full((8, TILE), NEG, jnp.float32)
            for c in range(t + 1):
                s = w["raw"][c * TILE:(c + 1) * TILE] * (scale * LOG2E) + bias(t, c)
                if c == t:
                    s = jnp.where(causal, s, NEG)
                score[slot, rows(c, TILE), :] = s
                top = jnp.maximum(top, fold(s, jnp.max))
            w["top"] = jnp.max(top, axis=0, keepdims=True)
        for w in work:
            w["pull"] = dot(v_all[group, w["span"], :], w["g_tr"])
        for w in work:
            t, slot = w["t"], w["slot"]
            total = jnp.zeros((8, TILE), jnp.float32)
            for c in range(t + 1):
                at = rows(c, TILE)
                e = jnp.exp2(score[slot, at, :] - w["top"])
                score[slot, at, :] = e
                p_low[slot, at, :] = e.astype(jnp.bfloat16)
                total = total + fold(e, jnp.sum)
            w["total"] = jnp.sum(total, axis=0, keepdims=True)
            w["out"] = dot(v_tr[group, :, w["span"]], p_low[slot, w["span"], :])
        square = jnp.zeros((1, TILE), jnp.float32)
        for w in work:
            t, slot = w["t"], w["slot"]
            inverse = 1.0 / w["total"]
            out = (w["out"] * inverse).astype(jnp.bfloat16).astype(jnp.float32)
            delta = jnp.sum(w["g_f32"] * out, axis=0, keepdims=True)
            log_norm = w["top"] * LN2 + jnp.log(w["total"])
            shift = delta - (2.0 * ZLOSS) * log_norm
            square = square + log_norm * log_norm
            for c in range(t + 1):
                at = rows(c, TILE)
                p = score[slot, at, :] * inverse
                ds = p * (w["pull"][c * TILE:(c + 1) * TILE] - shift)
                p_low[slot, at, :] = p.astype(jnp.bfloat16)
                ds_low[slot, at, :] = ds.astype(jnp.bfloat16)
        for w in work:
            slot, span = w["slot"], w["span"]
            dv_acc[group, span, :] += dot(p_low[slot, span, :], w["g"])
            dk_acc[group, span, :] += dot(ds_low[slot, span, :], w["q"])
            dq = dot(k_tr[group, :, span], ds_low[slot, span, :])
            dq_buf[item, rows(slot, TILE), :] = (dq * scale).T.astype(jnp.bfloat16)
        z_own[group, pl.ds(lax.rem(head, per), 1), :] += square[:, :BLK] + square[:, BLK:]

    def one_item(group, m):
        item = 2 * m + group
        half = y if group == 0 else x
        head_kv = kv_head(group, me)
        head = head_kv * per + m
        low = 2 * y if group == 0 else x
        high = 2 * y + 1 if group == 0 else 2 + x

        @pl.when(m == 0)
        def _():
            prepare(group, high)

        for slot in range(2):
            wait_for(q_all.at[item, rows(slot, TILE)], q_sem.at[item * 2 + slot])
            wait_for(g_all.at[item, rows(slot, TILE)], g_sem.at[item * 2 + slot])
        for choice, pair in enumerate(((0, 1), (2, 3)) if group == 0 else ((0, 2), (1, 3))):
            @pl.when(half == choice)
            def _(pair=pair):
                tile_pair(pair, group, head, item)

        def give_dq(i, c):
            tile = jnp.where(i < 2, high, low)
            part = lax.rem(i, 2)
            slot = 1 - i // 2
            move(dq_buf.at[item, rows(2 * slot + part, tok)], dq_out.at[0, :, lanes(head)],
                 send_sem.at[6], dq_sem.at[0], 2 * tile + part)
            return c

        lax.fori_loop(0, 4, give_dq, 0)

        @pl.when(m == per - 1)
        def _():
            sem = group * 2 + half
            col = lanes(head_kv)

            def give(c, carry):
                keys_at = rows(c, TILE)
                dk_buf[group, keys_at, :] = (dk_acc[group, keys_at, :] * scale).astype(jnp.bfloat16)
                dv_buf[group, keys_at, :] = dv_acc[group, keys_at, :].astype(jnp.bfloat16)
                for part in range(2):
                    to = 2 * c + part
                    move(dk_buf.at[group, rows(to, tok)], dk_part.at[half, :, col],
                         send_sem.at[7 + group], dk_sem.at[sem], to)
                    move(dv_buf.at[group, rows(to, tok)], dv_part.at[half, :, col],
                         send_sem.at[9 + group], dv_sem.at[sem], to)
                return carry

            lax.fori_loop(0, high + 1, give, 0)

    def one_step(m, carry):
        one_item(0, m)
        one_item(1, m)
        return carry

    lax.fori_loop(0, per, one_step, 0)

    move(z_own.at[0], z_set.at[y], z_sem.at[0], z_sem.at[2 + y], kv_head(0, me))
    move(z_own.at[1], z_set.at[x], z_sem.at[1], z_sem.at[2 + x], kv_head(1, me))
    wait_for(z_set.at[0], z_sem.at[2])
    wait_for(z_set.at[1], z_sem.at[3])
    z_all[my_dp] = z_set[0] + z_set[1]

    def send_z(j, c):
        pltpu.make_async_remote_copy(
            src_ref=z_all.at[my_dp], dst_ref=z_all.at[my_dp],
            send_sem=z_sem.at[4], recv_sem=z_sem.at[5],
            device_id=(lax.rem(my_dp + j, dp), me), device_id_type=MESH,
        ).start()
        return c

    lax.fori_loop(1, dp, send_z, 0)
    wait_for(z_all.at[pl.ds(0, dp - 1)], z_sem.at[5])
    z_sum = jnp.sum(jnp.sum(z_all[...], axis=0), axis=1, keepdims=True)
    z_out[...] = jnp.broadcast_to(z_sum * (ZLOSS / (seq * dp)), z_out.shape)

    for group in range(2):
        cols = pl.ds(group * 4 * HD, 4 * HD)
        both = (y == 0) if group == 0 else (chip < 3)
        for part, sems, result in ((dk_part, dk_sem, dk_out), (dv_part, dv_sem, dv_out)):
            wait_for(part.at[1, :, cols], sems.at[group * 2 + 1])

            @pl.when(both)
            def _(part=part, sems=sems, result=result):
                wait_for(part.at[0, :, cols], sems.at[group * 2])
                result[0, :, cols] = (
                    part[0, :, cols].astype(jnp.float32) + part[1, :, cols].astype(jnp.float32)
                ).astype(jnp.bfloat16)

            @pl.when(jnp.logical_not(both))
            def _(part=part, result=result):
                result[0, :, cols] = part[1, :, cols]

    wait_for(dq_out, dq_sem.at[0])

    def sent(ref, sem, count):
        wait_for(ref.at[pl.ds(0, count * tok)], sem)

    for group in range(2):
        late = (y == 1) if group == 0 else (chip == 3)
        for sem in (group, 2 + group):
            @pl.when(late)
            def _(sem=sem):
                sent(k_all.at[0], send_sem.at[sem], 3)

            @pl.when(jnp.logical_not(late))
            def _(sem=sem):
                sent(k_all.at[0], send_sem.at[sem], 7)

        whole = (y == 1) if group == 0 else (x == 1)
        for sem in (7 + group, 9 + group):
            @pl.when(whole)
            def _(sem=sem):
                sent(k_all.at[0], send_sem.at[sem], 7)

            @pl.when(jnp.logical_not(whole))
            def _(sem=sem):
                sent(k_all.at[0], send_sem.at[sem], 3 if group == 0 else 5)

        @pl.when(kv_head(group, me) != me)
        def _():
            wait_for(z_own.at[group], z_sem.at[group])

    wide = pl.ds(0, 24 * HD)
    for sem in (4, 5, 6):
        wait_for(dq_out.at[0, :, wide], send_sem.at[sem])
    wait_for(z_all.at[pl.ds(0, dp - 1)], z_sem.at[4])


def finish_kernel(dq, dk, dv, z, dq_out, dk_out, dv_out, z_out, sem):
    copies = [
        pltpu.make_async_copy(a, b, sem.at[i])
        for i, (a, b) in enumerate(((dq, dq_out), (dk, dk_out), (dv, dv_out)))
    ]
    for copy in copies:
        copy.start()
    for h in range(z_out.shape[0]):
        z_out[h] = z[h, 0]
    for copy in copies:
        copy.wait()


def quad_body(queries, keys, values, out_grad, block_mask):
    dp = lax.axis_size("dp")
    seq, items = 8 * BLK, 8
    low, wide = jnp.bfloat16, jnp.float32
    hbm = pl.BlockSpec(memory_space=pltpu.HBM)
    vmem = pl.BlockSpec(memory_space=pltpu.VMEM)
    smem = pl.BlockSpec(memory_space=pltpu.SMEM)
    shape = jax.ShapeDtypeStruct
    results = pl.pallas_call(
        functools.partial(quad_kernel, dp),
        out_shape=(
            shape(queries.shape, low), shape(keys.shape, low), shape(keys.shape, low),
            shape((8, BLK), wide),
        ),
        in_specs=[smem] + [hbm] * 4,
        out_specs=(hbm, vmem, vmem, vmem),
        scratch_shapes=[
            pltpu.VMEM((items, 2 * TILE, HD), low),
            pltpu.VMEM((items, 2 * TILE, HD), low),
            pltpu.VMEM((2, seq, HD), low),
            pltpu.VMEM((2, seq, HD), low),
            pltpu.VMEM((2, HD, seq), low),
            pltpu.VMEM((2, HD, seq), low),
            pltpu.VMEM((2, seq, TILE), wide),
            pltpu.VMEM((2, seq, TILE), low),
            pltpu.VMEM((2, seq, TILE), low),
            pltpu.VMEM((2, seq, HD), wide),
            pltpu.VMEM((2, seq, HD), wide),
            pltpu.VMEM((items, 2 * TILE, HD), low),
            pltpu.VMEM((2, seq, HD), low),
            pltpu.VMEM((2, seq, HD), low),
            pltpu.VMEM((2, BLK, KVH * HD), low),
            pltpu.VMEM((2, BLK, KVH * HD), low),
            pltpu.VMEM((2, 8, BLK), wide),
            pltpu.VMEM((2, 8, BLK), wide),
            pltpu.VMEM((dp, 8, BLK), wide),
            pltpu.SemaphoreType.DMA((2 * items,)),
            pltpu.SemaphoreType.DMA((2 * items,)),
            pltpu.SemaphoreType.DMA((8,)),
            pltpu.SemaphoreType.DMA((8,)),
            pltpu.SemaphoreType.DMA((1,)),
            pltpu.SemaphoreType.DMA((4,)),
            pltpu.SemaphoreType.DMA((4,)),
            pltpu.SemaphoreType.DMA((11,)),
            pltpu.SemaphoreType.DMA((6,)),
        ],
        compiler_params=pltpu.CompilerParams(
            collective_id=0, has_side_effects=True, vmem_limit_bytes=60 * 1024 * 1024
        ),
        name="attention_exchange",
    )(block_mask.transpose(1, 2, 0), queries, out_grad, keys, values)
    return pl.pallas_call(
        finish_kernel,
        out_shape=(
            shape(queries.shape, low), shape(keys.shape, low), shape(keys.shape, low),
            shape((H // 8,), wide),
        ),
        in_specs=[vmem, vmem, vmem, smem],
        out_specs=(hbm, hbm, hbm, smem),
        scratch_shapes=[pltpu.SemaphoreType.DMA((3,))],
        compiler_params=pltpu.CompilerParams(vmem_limit_bytes=62 * 1024 * 1024),
        name="write_results",
    )(*results)


def solution(mesh):
    quad = mesh.shape["ctx"] == 8
    return jax.shard_map(
        quad_body if quad else body,
        mesh=mesh,
        in_specs=(
            P("dp", "ctx", None),
            P("dp", "ctx", None),
            P("dp", "ctx", None),
            P("dp", "ctx", None),
            P(),
        ),
        out_specs=(P("dp", "ctx", None), P("dp", "ctx", None), P("dp", "ctx", None), P("ctx")),
        check_vma=False,
    )
```

```python
import functools
import math

import jax
import jax.numpy as jnp
from jax import lax
from jax.experimental import pallas as pl
from jax.experimental.pallas import tpu as pltpu
from jax.sharding import PartitionSpec as P

H = 32
KVH = 8
HD = 128
BLK = 128
ZLOSS = 0.05
NEG = -1e30
TILE = 2 * BLK
MESH = pl.DeviceIdType.MESH
LOG2E = math.log2(math.e)
LN2 = math.log(2.0)


def dot(a, b):
    return jnp.dot(a, b, preferred_element_type=jnp.float32)


def steps(count, step, state):
    if isinstance(count, int) and count <= 4:
        for i in range(count):
            state = step(i, state)
        return state
    return lax.fori_loop(0, count, step, state)


def rows(i, size):
    return pl.ds(i * size if isinstance(i, int) else pl.multiple_of(i * size, size), size)


def fold(x, op):
    return op(x.reshape(x.shape[0] // 8, 8, x.shape[1]), axis=0)


def kernel(
    sizes,
    mask, q_in, g_in, k_in, v_in,
    dq_out, dk_out, dv_out, z_out,
    q_all, g_all, k_all, v_all, k_tr, v_tr,
    score, dk_acc, dv_acc, dq_buf, dk_buf, dv_buf, z_own, z_all,
    q_sem, g_sem, kv_sem, out_sem, send_sem, z_sem,
):
    n, dp, per, share, tok = sizes
    seq = n * tok
    tiles = seq // TILE
    me = lax.axis_index("ctx")
    my_dp = lax.axis_index("dp")
    group = H // KVH
    scale = HD ** (-0.5)

    barrier = pltpu.get_barrier_semaphore()

    def greet(j, c):
        pl.semaphore_signal(
            barrier, inc=1, device_id=(my_dp, lax.rem(me + j, n)), device_id_type=MESH
        )
        return c

    def greet_dp(j, c):
        pl.semaphore_signal(
            barrier, inc=1, device_id=(lax.rem(my_dp + j, dp), me), device_id_type=MESH
        )
        return c

    lax.fori_loop(1, n, greet, 0)
    lax.fori_loop(1, dp, greet_dp, 0)
    pl.semaphore_wait(barrier, n - 1 + dp - 1)

    def lanes(i):
        return pl.ds(pl.multiple_of(i * HD, HD), HD)

    def remote(src, dst, send, recv, target):
        pltpu.make_async_remote_copy(
            src_ref=src, dst_ref=dst, send_sem=send, recv_sem=recv,
            device_id=(my_dp, target), device_id_type=MESH,
        ).start()

    mine = rows(me, tok)

    def kv_head(device):
        return (device * per) // group

    def send_kv(j, c):
        to = lax.rem(me + j, n)
        col = lanes(kv_head(to))
        remote(k_in.at[0, :, col], k_all.at[mine], send_sem.at[0], kv_sem.at[0], to)
        remote(v_in.at[0, :, col], v_all.at[mine], send_sem.at[1], kv_sem.at[1], to)
        return c

    lax.fori_loop(1, n, send_kv, 0)
    own = lanes(kv_head(me))
    pltpu.make_async_copy(k_in.at[0, :, own], k_all.at[mine], kv_sem.at[0]).start()
    pltpu.make_async_copy(v_in.at[0, :, own], v_all.at[mine], kv_sem.at[1]).start()

    def send_head(h, c):
        def send_q(j, c):
            to = lax.rem(me + j, n)
            col = lanes(to * per + h)
            remote(q_in.at[0, :, col], q_all.at[h, mine], send_sem.at[2], q_sem.at[h], to)
            remote(g_in.at[0, :, col], g_all.at[h, mine], send_sem.at[3], g_sem.at[h], to)
            return c

        lax.fori_loop(1, n, send_q, 0)
        col = lanes(me * per + h)
        pltpu.make_async_copy(q_in.at[0, :, col], q_all.at[h, mine], q_sem.at[h]).start()
        pltpu.make_async_copy(g_in.at[0, :, col], g_all.at[h, mine], g_sem.at[h]).start()
        return c

    lax.fori_loop(0, per, send_head, 0)

    def wait_for(ref, sem):
        pltpu.make_async_copy(ref, ref, sem).wait()

    z_own[...] = jnp.zeros_like(z_own)
    dk_acc[...] = jnp.zeros_like(dk_acc)
    dv_acc[...] = jnp.zeros_like(dv_acc)
    wait_for(k_all, kv_sem.at[0])
    wait_for(v_all, kv_sem.at[1])

    def turn(c, s):
        at = rows(c, TILE)
        k_tr[:, at] = k_all[at].astype(jnp.float32).T.astype(jnp.bfloat16)
        v_tr[:, at] = v_all[at].astype(jnp.float32).T.astype(jnp.bfloat16)
        return s

    steps(tiles, turn, 0)
    first_half = lax.broadcasted_iota(jnp.int32, (1, TILE), 1) < BLK
    causal = lax.broadcasted_iota(jnp.int32, (TILE, TILE), 0) <= lax.broadcasted_iota(
        jnp.int32, (TILE, TILE), 1
    )

    def one_head(h, c):
        wait_for(q_all.at[h], q_sem.at[h])
        wait_for(g_all.at[h], g_sem.at[h])
        head = me * per + h

        def one_tile(t):
            q_at = rows(t, TILE)
            q = q_all[h, q_at, :]
            g = g_all[h, q_at, :]
            q_tr = q.astype(jnp.float32).T.astype(jnp.bfloat16)
            g_f32 = g.astype(jnp.float32).T
            g_tr = g_f32.astype(jnp.bfloat16)

            def bias(c):
                parts = []
                for b in range(2):
                    left = mask[2 * t, 2 * c + b, head]
                    right = mask[2 * t + 1, 2 * c + b, head]
                    on = jnp.where(first_half, left, right).astype(jnp.float32)
                    parts.append(jnp.broadcast_to((1.0 - on) * NEG, (BLK, TILE)))
                return jnp.concatenate(parts, axis=0)

            def score_chunk(c, top, diagonal):
                at = rows(c, TILE)
                s = dot(k_all[at], q_tr) * (scale * LOG2E) + bias(c)
                if diagonal:
                    s = jnp.where(causal, s, NEG)
                score[at] = s
                return jnp.maximum(top, fold(s, jnp.max))

            top = jnp.full((8, TILE), NEG, jnp.float32)
            top = steps(t, lambda c, x: score_chunk(c, x, False), top)
            top = score_chunk(t, top, True)
            top = jnp.max(top, axis=0, keepdims=True)

            def exp_chunk(c, state):
                total, out = state
                at = rows(c, TILE)
                e = jnp.exp2(score[at] - top)
                score[at] = e
                out = out + dot(v_tr[:, at], e.astype(jnp.bfloat16))
                return total + fold(e, jnp.sum), out

            total, out = steps(
                t + 1, exp_chunk,
                (jnp.zeros((8, TILE), jnp.float32), jnp.zeros((HD, TILE), jnp.float32)),
            )
            total = jnp.sum(total, axis=0, keepdims=True)
            inverse = 1.0 / total
            out = (out * inverse).astype(jnp.bfloat16).astype(jnp.float32)
            delta = jnp.sum(g_f32 * out, axis=0, keepdims=True)
            log_norm = top * LN2 + jnp.log(total)
            shift = delta - (2.0 * ZLOSS) * log_norm
            square = log_norm * log_norm
            z_own[pl.ds(h, 1), :] += square[:, :BLK] + square[:, BLK:]

            def grad_chunk(c, dq):
                at = rows(c, TILE)
                p = score[at] * inverse
                dv_acc[at] += dot(p.astype(jnp.bfloat16), g)
                ds = (p * (dot(v_all[at], g_tr) - shift)).astype(jnp.bfloat16)
                dk_acc[at] += dot(ds, q)
                return dq + dot(k_tr[:, at], ds)

            dq = steps(t + 1, grad_chunk, jnp.zeros((HD, TILE), jnp.float32))
            dq_buf[h, q_at, :] = (dq * scale).T.astype(jnp.bfloat16)

            for part in range(TILE // tok):
                to = t * (TILE // tok) + part
                src = dq_buf.at[h, rows(to, tok)]
                dst = dq_out.at[0, :, lanes(head)]

                @pl.when(me == to)
                def _():
                    pltpu.make_async_copy(src, dst, out_sem.at[0]).start()

                @pl.when(me != to)
                def _():
                    remote(src, dst, send_sem.at[4], out_sem.at[0], to)

            @pl.when(h == per - 1)
            def _():
                dk_buf[q_at] = (dk_acc[q_at] * scale).astype(jnp.bfloat16)
                dv_buf[q_at] = dv_acc[q_at].astype(jnp.bfloat16)
                slot = lax.rem(me, share)
                col = lanes(kv_head(me))
                for part in range(TILE // tok):
                    to = t * (TILE // tok) + part
                    src_k = dk_buf.at[rows(to, tok)]
                    src_v = dv_buf.at[rows(to, tok)]

                    @pl.when(me == to)
                    def _():
                        pltpu.make_async_copy(src_k, dk_out.at[slot, :, col], out_sem.at[1]).start()
                        pltpu.make_async_copy(src_v, dv_out.at[slot, :, col], out_sem.at[2]).start()

                    @pl.when(me != to)
                    def _():
                        remote(src_k, dk_out.at[slot, :, col], send_sem.at[5], out_sem.at[1], to)
                        remote(src_v, dv_out.at[slot, :, col], send_sem.at[6], out_sem.at[2], to)

        if tiles <= 4:
            for t in reversed(range(tiles)):
                one_tile(t)
        else:
            def tile_step(i, s):
                one_tile(tiles - 1 - i)
                return s

            lax.fori_loop(0, tiles, tile_step, 0)
        return c

    lax.fori_loop(0, per, one_head, 0)

    pltpu.make_async_copy(z_own, z_all.at[my_dp], z_sem.at[1]).start()

    def send_z(j, c):
        pltpu.make_async_remote_copy(
            src_ref=z_own, dst_ref=z_all.at[my_dp], send_sem=z_sem.at[0], recv_sem=z_sem.at[1],
            device_id=(lax.rem(my_dp + j, dp), me), device_id_type=MESH,
        ).start()
        return c

    lax.fori_loop(1, dp, send_z, 0)
    wait_for(z_all, z_sem.at[1])
    z_sum = jnp.sum(jnp.sum(z_all[...], axis=0), axis=1, keepdims=True)
    z_out[...] = jnp.broadcast_to(z_sum * (ZLOSS / (seq * dp)), z_out.shape)

    wait_for(dq_out, out_sem.at[0])
    wait_for(dk_out, out_sem.at[1])
    wait_for(dv_out, out_sem.at[2])
    others = pl.ds(0, seq - tok)
    wide = pl.ds(0, (n - 1) * per * HD)
    wait_for(k_all.at[others], send_sem.at[0])
    wait_for(v_all.at[others], send_sem.at[1])
    wait_for(q_in.at[0, :, wide], send_sem.at[2])
    wait_for(g_in.at[0, :, wide], send_sem.at[3])
    wait_for(dq_out.at[0, :, wide], send_sem.at[4])
    wait_for(dk_buf.at[others], send_sem.at[5])
    wait_for(dv_buf.at[others], send_sem.at[6])
    wait_for(z_all.at[pl.ds(0, dp - 1)], z_sem.at[0])


def body(queries, keys, values, out_grad, block_mask):
    tok = queries.shape[1]
    n = lax.axis_size("ctx")
    dp = lax.axis_size("dp")
    per = H // n
    share = max(1, n // KVH)
    seq = tok * n
    low, wide = jnp.bfloat16, jnp.float32
    anywhere = pl.BlockSpec(memory_space=pl.ANY)
    dq, dk, dv, z = pl.pallas_call(
        functools.partial(kernel, (n, dp, per, share, tok)),
        out_shape=(
            jax.ShapeDtypeStruct(queries.shape, low),
            jax.ShapeDtypeStruct((share, tok, KVH * HD), low),
            jax.ShapeDtypeStruct((share, tok, KVH * HD), low),
            jax.ShapeDtypeStruct((8, BLK), wide),
        ),
        in_specs=[pl.BlockSpec(memory_space=pltpu.SMEM)] + [anywhere] * 4,
        out_specs=(anywhere, anywhere, anywhere, pl.BlockSpec(memory_space=pltpu.VMEM)),
        scratch_shapes=[
            pltpu.VMEM((per, seq, HD), low),
            pltpu.VMEM((per, seq, HD), low),
            pltpu.VMEM((seq, HD), low),
            pltpu.VMEM((seq, HD), low),
            pltpu.VMEM((HD, seq), low),
            pltpu.VMEM((HD, seq), low),
            pltpu.VMEM((seq, TILE), wide),
            pltpu.VMEM((seq, HD), wide),
            pltpu.VMEM((seq, HD), wide),
            pltpu.VMEM((per, seq, HD), low),
            pltpu.VMEM((seq, HD), low),
            pltpu.VMEM((seq, HD), low),
            pltpu.VMEM((8, BLK), wide),
            pltpu.VMEM((dp, 8, BLK), wide),
            pltpu.SemaphoreType.DMA((per,)),
            pltpu.SemaphoreType.DMA((per,)),
            pltpu.SemaphoreType.DMA((2,)),
            pltpu.SemaphoreType.DMA((3,)),
            pltpu.SemaphoreType.DMA((7,)),
            pltpu.SemaphoreType.DMA((2,)),
        ],
        compiler_params=pltpu.CompilerParams(
            collective_id=0, has_side_effects=True, vmem_limit_bytes=62 * 1024 * 1024
        ),
        name="attention_exchange",
    )(block_mask.transpose(1, 2, 0), queries, out_grad, keys, values)
    if share > 1:
        dk = jnp.sum(dk.astype(wide), axis=0, keepdims=True).astype(low)
        dv = jnp.sum(dv.astype(wide), axis=0, keepdims=True).astype(low)
    return (dq, dk, dv, z[:per, 0])


def quad_kernel(
    dp,
    mask, q_in, g_in, k_in, v_in,
    dq_out, dk_out, dv_out, z_out,
    q_all, g_all, k_all, v_all, k_tr, v_tr,
    score, p_low, ds_low, dk_acc, dv_acc, dq_buf, dk_buf, dv_buf, dk_part, dv_part, z_own, z_set, z_all,
    q_sem, g_sem, k_sem, v_sem, dq_sem, dk_sem, dv_sem, send_sem, z_sem,
):
    n, tok, per = 8, BLK, H // KVH
    seq = n * tok
    me = lax.axis_index("ctx")
    my_dp = lax.axis_index("dp")
    y, x, core = me // 4, lax.rem(me // 2, 2), lax.rem(me, 2)
    chip = me // 2
    scale = HD ** (-0.5)

    barrier = pltpu.get_barrier_semaphore()

    def greet(j, c):
        pl.semaphore_signal(
            barrier, inc=1, device_id=(my_dp, lax.rem(me + j, n)), device_id_type=MESH
        )
        return c

    def greet_dp(j, c):
        pl.semaphore_signal(
            barrier, inc=1, device_id=(lax.rem(my_dp + j, dp), me), device_id_type=MESH
        )
        return c

    lax.fori_loop(1, n, greet, 0)
    lax.fori_loop(1, dp, greet_dp, 0)
    pl.semaphore_wait(barrier, n - 1 + dp - 1)

    def lanes(i):
        return pl.ds(pl.multiple_of(i * HD, HD), HD)

    def remote(src, dst, send, recv, target):
        pltpu.make_async_remote_copy(
            src_ref=src, dst_ref=dst, send_sem=send, recv_sem=recv,
            device_id=(my_dp, target), device_id_type=MESH,
        ).start()

    def move(src, dst, send, recv, target):
        @pl.when(target == me)
        def _():
            pltpu.make_async_copy(src, dst, recv).start()

        @pl.when(target != me)
        def _():
            remote(src, dst, send, recv, target)

    def wait_for(ref, sem):
        pltpu.make_async_copy(ref, ref, sem).wait()

    def kv_head(group, to):
        first = 2 * lax.rem(to // 2, 2) + lax.rem(to, 2)
        second = 4 + 2 * (to // 4) + lax.rem(to, 2)
        return first if group == 0 else second

    mine = rows(me, tok)

    def send_kv(group):
        def one(j, c):
            to = lax.rem(me + j, n)
            last = 2 * (to // 4) + 1 if group == 0 else 2 + lax.rem(to // 2, 2)

            @pl.when(chip <= last)
            def _():
                col = lanes(kv_head(group, to))
                move(k_in.at[0, :, col], k_all.at[group, mine], send_sem.at[group],
                     k_sem.at[group * 4 + chip], to)
                move(v_in.at[0, :, col], v_all.at[group, mine], send_sem.at[2 + group],
                     v_sem.at[group * 4 + chip], to)

            return c

        lax.fori_loop(0, n, one, 0)

    def send_q(group, m):
        item = 2 * m + group
        slot = x if group == 0 else y
        place = rows(2 * slot + core, tok)

        def one(j, c):
            far = lax.rem((x if group == 0 else y) + j // 2, 2)
            to = 2 * far + lax.rem(core + j, 2) + (4 * y if group == 0 else 0)
            if group == 1:
                to = 4 * far + 2 * x + lax.rem(core + j, 2)
            col = lanes(kv_head(group, to) * per + m)
            at = item * 2 + slot
            move(q_in.at[0, :, col], q_all.at[item, place], send_sem.at[4], q_sem.at[at], to)
            move(g_in.at[0, :, col], g_all.at[item, place], send_sem.at[5], g_sem.at[at], to)
            return c

        lax.fori_loop(0, 4, one, 0)

    def send_pair(m, c):
        send_q(0, m)
        send_q(1, m)
        return c

    send_kv(0)
    send_q(0, 0)
    send_kv(1)
    send_q(1, 0)
    lax.fori_loop(1, per, send_pair, 0)

    z_own[...] = jnp.zeros_like(z_own)
    dk_acc[...] = jnp.zeros_like(dk_acc)
    dv_acc[...] = jnp.zeros_like(dv_acc)
    first_half = lax.broadcasted_iota(jnp.int32, (1, TILE), 1) < BLK
    causal = lax.broadcasted_iota(jnp.int32, (TILE, TILE), 0) <= lax.broadcasted_iota(
        jnp.int32, (TILE, TILE), 1
    )

    def prepare(group, last):
        def one(c, carry):
            at = rows(c, TILE)
            wait_for(k_all.at[group, at], k_sem.at[group * 4 + c])
            wait_for(v_all.at[group, at], v_sem.at[group * 4 + c])
            k_tr[group, :, at] = k_all[group, at, :].astype(jnp.float32).T.astype(jnp.bfloat16)
            v_tr[group, :, at] = v_all[group, at, :].astype(jnp.float32).T.astype(jnp.bfloat16)
            return carry

        lax.fori_loop(0, last + 1, one, 0)

    def tile_pair(pair, group, head, item):
        work = []
        for slot, t in ((1, pair[1]), (0, pair[0])):
            q = q_all[item, rows(slot, TILE), :]
            g = g_all[item, rows(slot, TILE), :]
            g_f32 = g.astype(jnp.float32).T
            work.append(dict(
                slot=slot, t=t, span=pl.ds(0, (t + 1) * TILE), q=q, g=g, g_f32=g_f32,
                q_tr=q.astype(jnp.float32).T.astype(jnp.bfloat16), g_tr=g_f32.astype(jnp.bfloat16),
            ))

        def bias(t, block):
            left = mask[2 * t, block, head]
            right = mask[2 * t + 1, block, head]
            on = jnp.where(first_half, left, right).astype(jnp.float32)
            return (1.0 - on) * NEG

        for w in work:
            t, slot = w["t"], w["slot"]
            top = jnp.full((8, TILE), NEG, jnp.float32)
            w["bias"] = [bias(t, block) for block in range(2 * t + 2)]
            for c in range(t + 1):
                at = rows(c, TILE)
                raw = dot(k_all[group, at, :], w["q_tr"])
                if c == t:
                    raw = jnp.where(causal, raw, NEG)
                score[slot, at, :] = raw
                for b in range(2):
                    best = fold(raw[b * BLK:(b + 1) * BLK], jnp.max) * (scale * LOG2E)
                    top = jnp.maximum(top, best + w["bias"][2 * c + b])
            w["top"] = jnp.max(top, axis=0, keepdims=True)
        for w in work:
            t, slot = w["t"], w["slot"]
            total = jnp.zeros((8, TILE), jnp.float32)
            for block in range(2 * t + 2):
                at = rows(block, BLK)
                e = jnp.exp2(
                    score[slot, at, :] * (scale * LOG2E) + (w["bias"][block] - w["top"])
                )
                score[slot, at, :] = e
                p_low[slot, at, :] = e.astype(jnp.bfloat16)
                total = total + fold(e, jnp.sum)
            w["total"] = jnp.sum(total, axis=0, keepdims=True)
            w["out"] = dot(v_tr[group, :, w["span"]], p_low[slot, w["span"], :])
        square = jnp.zeros((1, TILE), jnp.float32)
        for w in work:
            t, slot = w["t"], w["slot"]
            inverse = 1.0 / w["total"]
            out = (w["out"] * inverse).astype(jnp.bfloat16).astype(jnp.float32)
            delta = jnp.sum(w["g_f32"] * out, axis=0, keepdims=True)
            log_norm = w["top"] * LN2 + jnp.log(w["total"])
            shift = delta - (2.0 * ZLOSS) * log_norm
            square = square + log_norm * log_norm
            for c in range(t + 1):
                at = rows(c, TILE)
                p = score[slot, at, :] * inverse
                ds = p * (dot(v_all[group, at, :], w["g_tr"]) - shift)
                p_low[slot, at, :] = p.astype(jnp.bfloat16)
                ds_low[slot, at, :] = ds.astype(jnp.bfloat16)
        for w in work:
            slot, span = w["slot"], w["span"]
            dv_acc[group, span, :] += dot(p_low[slot, span, :], w["g"])
            dk_acc[group, span, :] += dot(ds_low[slot, span, :], w["q"])
            dq = dot(k_tr[group, :, span], ds_low[slot, span, :])
            dq_buf[item, rows(slot, TILE), :] = (dq * scale).T.astype(jnp.bfloat16)
        z_own[group, pl.ds(lax.rem(head, per), 1), :] += square[:, :BLK] + square[:, BLK:]

    def one_item(group, m):
        item = 2 * m + group
        half = y if group == 0 else x
        head_kv = kv_head(group, me)
        head = head_kv * per + m
        low = 2 * y if group == 0 else x
        high = 2 * y + 1 if group == 0 else 2 + x

        @pl.when(m == 0)
        def _():
            prepare(group, high)

        for slot in range(2):
            wait_for(q_all.at[item, rows(slot, TILE)], q_sem.at[item * 2 + slot])
            wait_for(g_all.at[item, rows(slot, TILE)], g_sem.at[item * 2 + slot])
        for choice, pair in enumerate(((0, 1), (2, 3)) if group == 0 else ((0, 2), (1, 3))):
            @pl.when(half == choice)
            def _(pair=pair):
                tile_pair(pair, group, head, item)

        def give_dq(i, c):
            tile = jnp.where(i < 2, high, low)
            part = lax.rem(i, 2)
            slot = 1 - i // 2
            move(dq_buf.at[item, rows(2 * slot + part, tok)], dq_out.at[0, :, lanes(head)],
                 send_sem.at[6], dq_sem.at[0], 2 * tile + part)
            return c

        lax.fori_loop(0, 4, give_dq, 0)

        @pl.when(m == per - 1)
        def _():
            sem = group * 2 + half
            col = lanes(head_kv)

            def give(c, carry):
                keys_at = rows(c, TILE)
                dk_buf[group, keys_at, :] = (dk_acc[group, keys_at, :] * scale).astype(jnp.bfloat16)
                dv_buf[group, keys_at, :] = dv_acc[group, keys_at, :].astype(jnp.bfloat16)
                for part in range(2):
                    to = 2 * c + part
                    move(dk_buf.at[group, rows(to, tok)], dk_part.at[half, :, col],
                         send_sem.at[7 + group], dk_sem.at[sem], to)
                    move(dv_buf.at[group, rows(to, tok)], dv_part.at[half, :, col],
                         send_sem.at[9 + group], dv_sem.at[sem], to)
                return carry

            lax.fori_loop(0, high + 1, give, 0)

    def one_step(m, carry):
        one_item(0, m)
        one_item(1, m)
        return carry

    lax.fori_loop(0, per, one_step, 0)

    move(z_own.at[0], z_set.at[y], z_sem.at[0], z_sem.at[2 + y], kv_head(0, me))
    move(z_own.at[1], z_set.at[x], z_sem.at[1], z_sem.at[2 + x], kv_head(1, me))
    wait_for(z_set.at[0], z_sem.at[2])
    wait_for(z_set.at[1], z_sem.at[3])
    z_all[my_dp] = z_set[0] + z_set[1]

    def send_z(j, c):
        pltpu.make_async_remote_copy(
            src_ref=z_all.at[my_dp], dst_ref=z_all.at[my_dp],
            send_sem=z_sem.at[4], recv_sem=z_sem.at[5],
            device_id=(lax.rem(my_dp + j, dp), me), device_id_type=MESH,
        ).start()
        return c

    lax.fori_loop(1, dp, send_z, 0)
    wait_for(z_all.at[pl.ds(0, dp - 1)], z_sem.at[5])
    z_sum = jnp.sum(jnp.sum(z_all[...], axis=0), axis=1, keepdims=True)
    z_out[...] = jnp.broadcast_to(z_sum * (ZLOSS / (seq * dp)), z_out.shape)

    for group in range(2):
        cols = pl.ds(group * 4 * HD, 4 * HD)
        both = (y == 0) if group == 0 else (chip < 3)
        for part, sems, result in ((dk_part, dk_sem, dk_out), (dv_part, dv_sem, dv_out)):
            wait_for(part.at[1, :, cols], sems.at[group * 2 + 1])

            @pl.when(both)
            def _(part=part, sems=sems, result=result):
                wait_for(part.at[0, :, cols], sems.at[group * 2])
                result[0, :, cols] = (
                    part[0, :, cols].astype(jnp.float32) + part[1, :, cols].astype(jnp.float32)
                ).astype(jnp.bfloat16)

            @pl.when(jnp.logical_not(both))
            def _(part=part, result=result):
                result[0, :, cols] = part[1, :, cols]

    wait_for(dq_out, dq_sem.at[0])

    def sent(ref, sem, count):
        wait_for(ref.at[pl.ds(0, count * tok)], sem)

    for group in range(2):
        late = (y == 1) if group == 0 else (chip == 3)
        for sem in (group, 2 + group):
            @pl.when(late)
            def _(sem=sem):
                sent(k_all.at[0], send_sem.at[sem], 3)

            @pl.when(jnp.logical_not(late))
            def _(sem=sem):
                sent(k_all.at[0], send_sem.at[sem], 7)

        whole = (y == 1) if group == 0 else (x == 1)
        for sem in (7 + group, 9 + group):
            @pl.when(whole)
            def _(sem=sem):
                sent(k_all.at[0], send_sem.at[sem], 7)

            @pl.when(jnp.logical_not(whole))
            def _(sem=sem):
                sent(k_all.at[0], send_sem.at[sem], 3 if group == 0 else 5)

        @pl.when(kv_head(group, me) != me)
        def _():
            wait_for(z_own.at[group], z_sem.at[group])

    wide = pl.ds(0, 24 * HD)
    for sem in (4, 5, 6):
        wait_for(dq_out.at[0, :, wide], send_sem.at[sem])
    wait_for(z_all.at[pl.ds(0, dp - 1)], z_sem.at[4])


def finish_kernel(
    dq, dk, dv, z, dq_out, dk_out, dv_out, z_out, dq_buf, dk_buf, dv_buf, in_sem, out_sem
):
    first, second = [], []
    for src, buf, dst, parts in (
        (dq, dq_buf, dq_out, 4), (dk, dk_buf, dk_out, 1), (dv, dv_buf, dv_out, 1)
    ):
        size = src.shape[1] // parts
        for i in range(parts):
            at, k = pl.ds(i * size, size), len(first)
            first.append(pltpu.make_async_copy(src.at[:, at], buf.at[:, at], in_sem.at[k]))
            second.append(pltpu.make_async_copy(buf.at[:, at], dst.at[:, at], out_sem.at[k]))
    for copy in first:
        copy.start()
    for h in range(z_out.shape[0]):
        z_out[h] = z[h, 0]
    for before, after in zip(first, second):
        before.wait()
        after.start()
    for copy in second:
        copy.wait()


def quad_body(queries, keys, values, out_grad, block_mask):
    dp = lax.axis_size("dp")
    seq, items = 8 * BLK, 8
    low, wide = jnp.bfloat16, jnp.float32
    hbm = pl.BlockSpec(memory_space=pltpu.HBM)
    vmem = pl.BlockSpec(memory_space=pltpu.VMEM)
    smem = pl.BlockSpec(memory_space=pltpu.SMEM)
    shape = jax.ShapeDtypeStruct
    results = pl.pallas_call(
        functools.partial(quad_kernel, dp),
        out_shape=(
            shape(queries.shape, low), shape(keys.shape, low), shape(keys.shape, low),
            shape((8, BLK), wide),
        ),
        in_specs=[smem] + [hbm] * 4,
        out_specs=(hbm, vmem, vmem, vmem),
        scratch_shapes=[
            pltpu.VMEM((items, 2 * TILE, HD), low),
            pltpu.VMEM((items, 2 * TILE, HD), low),
            pltpu.VMEM((2, seq, HD), low),
            pltpu.VMEM((2, seq, HD), low),
            pltpu.VMEM((2, HD, seq), low),
            pltpu.VMEM((2, HD, seq), low),
            pltpu.VMEM((2, seq, TILE), wide),
            pltpu.VMEM((2, seq, TILE), low),
            pltpu.VMEM((2, seq, TILE), low),
            pltpu.VMEM((2, seq, HD), wide),
            pltpu.VMEM((2, seq, HD), wide),
            pltpu.VMEM((items, 2 * TILE, HD), low),
            pltpu.VMEM((2, seq, HD), low),
            pltpu.VMEM((2, seq, HD), low),
            pltpu.VMEM((2, BLK, KVH * HD), low),
            pltpu.VMEM((2, BLK, KVH * HD), low),
            pltpu.VMEM((2, 8, BLK), wide),
            pltpu.VMEM((2, 8, BLK), wide),
            pltpu.VMEM((dp, 8, BLK), wide),
            pltpu.SemaphoreType.DMA((2 * items,)),
            pltpu.SemaphoreType.DMA((2 * items,)),
            pltpu.SemaphoreType.DMA((8,)),
            pltpu.SemaphoreType.DMA((8,)),
            pltpu.SemaphoreType.DMA((1,)),
            pltpu.SemaphoreType.DMA((4,)),
            pltpu.SemaphoreType.DMA((4,)),
            pltpu.SemaphoreType.DMA((11,)),
            pltpu.SemaphoreType.DMA((6,)),
        ],
        compiler_params=pltpu.CompilerParams(
            collective_id=0, has_side_effects=True, vmem_limit_bytes=60 * 1024 * 1024
        ),
        name="attention_exchange",
    )(block_mask.transpose(1, 2, 0), queries, out_grad, keys, values)
    return pl.pallas_call(
        finish_kernel,
        out_shape=(
            shape(queries.shape, low), shape(keys.shape, low), shape(keys.shape, low),
            shape((H // 8,), wide),
        ),
        in_specs=[hbm, hbm, hbm, smem],
        out_specs=(hbm, hbm, hbm, smem),
        scratch_shapes=[
            pltpu.VMEM(queries.shape, low), pltpu.VMEM(keys.shape, low),
            pltpu.VMEM(keys.shape, low),
            pltpu.SemaphoreType.DMA((6,)), pltpu.SemaphoreType.DMA((6,)),
        ],
        compiler_params=pltpu.CompilerParams(vmem_limit_bytes=62 * 1024 * 1024),
        name="write_results",
    )(*results)


def solution(mesh):
    quad = mesh.shape["ctx"] == 8
    return jax.shard_map(
        quad_body if quad else body,
        mesh=mesh,
        in_specs=(
            P("dp", "ctx", None),
            P("dp", "ctx", None),
            P("dp", "ctx", None),
            P("dp", "ctx", None),
            P(),
        ),
        out_specs=(P("dp", "ctx", None), P("dp", "ctx", None), P("dp", "ctx", None), P("ctx")),
        check_vma=False,
    )
```

```python
import functools
import math

import jax
import jax.numpy as jnp
from jax import lax
from jax.experimental import pallas as pl
from jax.experimental.pallas import tpu as pltpu
from jax.sharding import PartitionSpec as P

H = 32
KVH = 8
HD = 128
BLK = 128
ZLOSS = 0.05
NEG = -1e30
TILE = 2 * BLK
MESH = pl.DeviceIdType.MESH
LOG2E = math.log2(math.e)
LN2 = math.log(2.0)


def dot(a, b):
    return jnp.dot(a, b, preferred_element_type=jnp.float32)


def steps(count, step, state):
    if isinstance(count, int) and count <= 4:
        for i in range(count):
            state = step(i, state)
        return state
    return lax.fori_loop(0, count, step, state)


def rows(i, size):
    return pl.ds(i * size if isinstance(i, int) else pl.multiple_of(i * size, size), size)


def fold(x, op):
    return op(x.reshape(x.shape[0] // 8, 8, x.shape[1]), axis=0)


def kernel(
    sizes,
    mask, q_in, g_in, k_in, v_in,
    dq_out, dk_out, dv_out, z_out,
    q_all, g_all, k_all, v_all, k_tr, v_tr,
    score, dk_acc, dv_acc, dq_buf, dk_buf, dv_buf, z_own, z_all,
    q_sem, g_sem, kv_sem, out_sem, send_sem, z_sem,
):
    n, dp, per, share, tok = sizes
    seq = n * tok
    tiles = seq // TILE
    me = lax.axis_index("ctx")
    my_dp = lax.axis_index("dp")
    group = H // KVH
    scale = HD ** (-0.5)

    barrier = pltpu.get_barrier_semaphore()

    def greet(j, c):
        pl.semaphore_signal(
            barrier, inc=1, device_id=(my_dp, lax.rem(me + j, n)), device_id_type=MESH
        )
        return c

    def greet_dp(j, c):
        pl.semaphore_signal(
            barrier, inc=1, device_id=(lax.rem(my_dp + j, dp), me), device_id_type=MESH
        )
        return c

    lax.fori_loop(1, n, greet, 0)
    lax.fori_loop(1, dp, greet_dp, 0)
    pl.semaphore_wait(barrier, n - 1 + dp - 1)

    def lanes(i):
        return pl.ds(pl.multiple_of(i * HD, HD), HD)

    def remote(src, dst, send, recv, target):
        pltpu.make_async_remote_copy(
            src_ref=src, dst_ref=dst, send_sem=send, recv_sem=recv,
            device_id=(my_dp, target), device_id_type=MESH,
        ).start()

    mine = rows(me, tok)

    def kv_head(device):
        return (device * per) // group

    def send_kv(j, c):
        to = lax.rem(me + j, n)
        col = lanes(kv_head(to))
        remote(k_in.at[0, :, col], k_all.at[mine], send_sem.at[0], kv_sem.at[0], to)
        remote(v_in.at[0, :, col], v_all.at[mine], send_sem.at[1], kv_sem.at[1], to)
        return c

    lax.fori_loop(1, n, send_kv, 0)
    own = lanes(kv_head(me))
    pltpu.make_async_copy(k_in.at[0, :, own], k_all.at[mine], kv_sem.at[0]).start()
    pltpu.make_async_copy(v_in.at[0, :, own], v_all.at[mine], kv_sem.at[1]).start()

    def send_head(h, c):
        def send_q(j, c):
            to = lax.rem(me + j, n)
            col = lanes(to * per + h)
            remote(q_in.at[0, :, col], q_all.at[h, mine], send_sem.at[2], q_sem.at[h], to)
            remote(g_in.at[0, :, col], g_all.at[h, mine], send_sem.at[3], g_sem.at[h], to)
            return c

        lax.fori_loop(1, n, send_q, 0)
        col = lanes(me * per + h)
        pltpu.make_async_copy(q_in.at[0, :, col], q_all.at[h, mine], q_sem.at[h]).start()
        pltpu.make_async_copy(g_in.at[0, :, col], g_all.at[h, mine], g_sem.at[h]).start()
        return c

    lax.fori_loop(0, per, send_head, 0)

    def wait_for(ref, sem):
        pltpu.make_async_copy(ref, ref, sem).wait()

    z_own[...] = jnp.zeros_like(z_own)
    dk_acc[...] = jnp.zeros_like(dk_acc)
    dv_acc[...] = jnp.zeros_like(dv_acc)
    wait_for(k_all, kv_sem.at[0])
    wait_for(v_all, kv_sem.at[1])

    def turn(c, s):
        at = rows(c, TILE)
        k_tr[:, at] = k_all[at].astype(jnp.float32).T.astype(jnp.bfloat16)
        v_tr[:, at] = v_all[at].astype(jnp.float32).T.astype(jnp.bfloat16)
        return s

    steps(tiles, turn, 0)
    first_half = lax.broadcasted_iota(jnp.int32, (1, TILE), 1) < BLK
    causal = lax.broadcasted_iota(jnp.int32, (TILE, TILE), 0) <= lax.broadcasted_iota(
        jnp.int32, (TILE, TILE), 1
    )

    def one_head(h, c):
        wait_for(q_all.at[h], q_sem.at[h])
        wait_for(g_all.at[h], g_sem.at[h])
        head = me * per + h

        def one_tile(t):
            q_at = rows(t, TILE)
            q = q_all[h, q_at, :]
            g = g_all[h, q_at, :]
            q_tr = q.astype(jnp.float32).T.astype(jnp.bfloat16)
            g_f32 = g.astype(jnp.float32).T
            g_tr = g_f32.astype(jnp.bfloat16)

            def bias(c):
                parts = []
                for b in range(2):
                    left = mask[2 * t, 2 * c + b, head]
                    right = mask[2 * t + 1, 2 * c + b, head]
                    on = jnp.where(first_half, left, right).astype(jnp.float32)
                    parts.append(jnp.broadcast_to((1.0 - on) * NEG, (BLK, TILE)))
                return jnp.concatenate(parts, axis=0)

            def score_chunk(c, top, diagonal):
                at = rows(c, TILE)
                s = dot(k_all[at], q_tr) * (scale * LOG2E) + bias(c)
                if diagonal:
                    s = jnp.where(causal, s, NEG)
                score[at] = s
                return jnp.maximum(top, fold(s, jnp.max))

            top = jnp.full((8, TILE), NEG, jnp.float32)
            top = steps(t, lambda c, x: score_chunk(c, x, False), top)
            top = score_chunk(t, top, True)
            top = jnp.max(top, axis=0, keepdims=True)

            def exp_chunk(c, state):
                total, out = state
                at = rows(c, TILE)
                e = jnp.exp2(score[at] - top)
                score[at] = e
                out = out + dot(v_tr[:, at], e.astype(jnp.bfloat16))
                return total + fold(e, jnp.sum), out

            total, out = steps(
                t + 1, exp_chunk,
                (jnp.zeros((8, TILE), jnp.float32), jnp.zeros((HD, TILE), jnp.float32)),
            )
            total = jnp.sum(total, axis=0, keepdims=True)
            inverse = 1.0 / total
            out = (out * inverse).astype(jnp.bfloat16).astype(jnp.float32)
            delta = jnp.sum(g_f32 * out, axis=0, keepdims=True)
            log_norm = top * LN2 + jnp.log(total)
            shift = delta - (2.0 * ZLOSS) * log_norm
            square = log_norm * log_norm
            z_own[pl.ds(h, 1), :] += square[:, :BLK] + square[:, BLK:]

            def grad_chunk(c, dq):
                at = rows(c, TILE)
                p = score[at] * inverse
                dv_acc[at] += dot(p.astype(jnp.bfloat16), g)
                ds = (p * (dot(v_all[at], g_tr) - shift)).astype(jnp.bfloat16)
                dk_acc[at] += dot(ds, q)
                return dq + dot(k_tr[:, at], ds)

            dq = steps(t + 1, grad_chunk, jnp.zeros((HD, TILE), jnp.float32))
            dq_buf[h, q_at, :] = (dq * scale).T.astype(jnp.bfloat16)

            for part in range(TILE // tok):
                to = t * (TILE // tok) + part
                src = dq_buf.at[h, rows(to, tok)]
                dst = dq_out.at[0, :, lanes(head)]

                @pl.when(me == to)
                def _():
                    pltpu.make_async_copy(src, dst, out_sem.at[0]).start()

                @pl.when(me != to)
                def _():
                    remote(src, dst, send_sem.at[4], out_sem.at[0], to)

            @pl.when(h == per - 1)
            def _():
                dk_buf[q_at] = (dk_acc[q_at] * scale).astype(jnp.bfloat16)
                dv_buf[q_at] = dv_acc[q_at].astype(jnp.bfloat16)
                slot = lax.rem(me, share)
                col = lanes(kv_head(me))
                for part in range(TILE // tok):
                    to = t * (TILE // tok) + part
                    src_k = dk_buf.at[rows(to, tok)]
                    src_v = dv_buf.at[rows(to, tok)]

                    @pl.when(me == to)
                    def _():
                        pltpu.make_async_copy(src_k, dk_out.at[slot, :, col], out_sem.at[1]).start()
                        pltpu.make_async_copy(src_v, dv_out.at[slot, :, col], out_sem.at[2]).start()

                    @pl.when(me != to)
                    def _():
                        remote(src_k, dk_out.at[slot, :, col], send_sem.at[5], out_sem.at[1], to)
                        remote(src_v, dv_out.at[slot, :, col], send_sem.at[6], out_sem.at[2], to)

        if tiles <= 4:
            for t in reversed(range(tiles)):
                one_tile(t)
        else:
            def tile_step(i, s):
                one_tile(tiles - 1 - i)
                return s

            lax.fori_loop(0, tiles, tile_step, 0)
        return c

    lax.fori_loop(0, per, one_head, 0)

    pltpu.make_async_copy(z_own, z_all.at[my_dp], z_sem.at[1]).start()

    def send_z(j, c):
        pltpu.make_async_remote_copy(
            src_ref=z_own, dst_ref=z_all.at[my_dp], send_sem=z_sem.at[0], recv_sem=z_sem.at[1],
            device_id=(lax.rem(my_dp + j, dp), me), device_id_type=MESH,
        ).start()
        return c

    lax.fori_loop(1, dp, send_z, 0)
    wait_for(z_all, z_sem.at[1])
    z_sum = jnp.sum(jnp.sum(z_all[...], axis=0), axis=1, keepdims=True)
    z_out[...] = jnp.broadcast_to(z_sum * (ZLOSS / (seq * dp)), z_out.shape)

    wait_for(dq_out, out_sem.at[0])
    wait_for(dk_out, out_sem.at[1])
    wait_for(dv_out, out_sem.at[2])
    others = pl.ds(0, seq - tok)
    wide = pl.ds(0, (n - 1) * per * HD)
    wait_for(k_all.at[others], send_sem.at[0])
    wait_for(v_all.at[others], send_sem.at[1])
    wait_for(q_in.at[0, :, wide], send_sem.at[2])
    wait_for(g_in.at[0, :, wide], send_sem.at[3])
    wait_for(dq_out.at[0, :, wide], send_sem.at[4])
    wait_for(dk_buf.at[others], send_sem.at[5])
    wait_for(dv_buf.at[others], send_sem.at[6])
    wait_for(z_all.at[pl.ds(0, dp - 1)], z_sem.at[0])


def body(queries, keys, values, out_grad, block_mask):
    tok = queries.shape[1]
    n = lax.axis_size("ctx")
    dp = lax.axis_size("dp")
    per = H // n
    share = max(1, n // KVH)
    seq = tok * n
    low, wide = jnp.bfloat16, jnp.float32
    anywhere = pl.BlockSpec(memory_space=pl.ANY)
    dq, dk, dv, z = pl.pallas_call(
        functools.partial(kernel, (n, dp, per, share, tok)),
        out_shape=(
            jax.ShapeDtypeStruct(queries.shape, low),
            jax.ShapeDtypeStruct((share, tok, KVH * HD), low),
            jax.ShapeDtypeStruct((share, tok, KVH * HD), low),
            jax.ShapeDtypeStruct((8, BLK), wide),
        ),
        in_specs=[pl.BlockSpec(memory_space=pltpu.SMEM)] + [anywhere] * 4,
        out_specs=(anywhere, anywhere, anywhere, pl.BlockSpec(memory_space=pltpu.VMEM)),
        scratch_shapes=[
            pltpu.VMEM((per, seq, HD), low),
            pltpu.VMEM((per, seq, HD), low),
            pltpu.VMEM((seq, HD), low),
            pltpu.VMEM((seq, HD), low),
            pltpu.VMEM((HD, seq), low),
            pltpu.VMEM((HD, seq), low),
            pltpu.VMEM((seq, TILE), wide),
            pltpu.VMEM((seq, HD), wide),
            pltpu.VMEM((seq, HD), wide),
            pltpu.VMEM((per, seq, HD), low),
            pltpu.VMEM((seq, HD), low),
            pltpu.VMEM((seq, HD), low),
            pltpu.VMEM((8, BLK), wide),
            pltpu.VMEM((dp, 8, BLK), wide),
            pltpu.SemaphoreType.DMA((per,)),
            pltpu.SemaphoreType.DMA((per,)),
            pltpu.SemaphoreType.DMA((2,)),
            pltpu.SemaphoreType.DMA((3,)),
            pltpu.SemaphoreType.DMA((7,)),
            pltpu.SemaphoreType.DMA((2,)),
        ],
        compiler_params=pltpu.CompilerParams(
            collective_id=0, has_side_effects=True, vmem_limit_bytes=62 * 1024 * 1024
        ),
        name="attention_exchange",
    )(block_mask.transpose(1, 2, 0), queries, out_grad, keys, values)
    if share > 1:
        dk = jnp.sum(dk.astype(wide), axis=0, keepdims=True).astype(low)
        dv = jnp.sum(dv.astype(wide), axis=0, keepdims=True).astype(low)
    return (dq, dk, dv, z[:per, 0])


def quad_kernel(
    dp,
    mask, q_in, g_in, k_in, v_in,
    dq_out, dk_out, dv_out, z_out,
    q_all, g_all, k_all, v_all, k_tr, v_tr,
    score, p_low, ds_low, dk_acc, dv_acc, dq_buf, dk_buf, dv_buf, dk_part, dv_part, z_own, z_set, z_all,
    q_sem, g_sem, k_sem, v_sem, dq_sem, dk_sem, dv_sem, send_sem, z_sem,
):
    n, tok, per = 8, BLK, H // KVH
    seq = n * tok
    me = lax.axis_index("ctx")
    my_dp = lax.axis_index("dp")
    y, x, core = me // 4, lax.rem(me // 2, 2), lax.rem(me, 2)
    chip = me // 2
    scale = HD ** (-0.5)

    barrier = pltpu.get_barrier_semaphore()

    def greet(j, c):
        pl.semaphore_signal(
            barrier, inc=1, device_id=(my_dp, lax.rem(me + j, n)), device_id_type=MESH
        )
        return c

    def greet_dp(j, c):
        pl.semaphore_signal(
            barrier, inc=1, device_id=(lax.rem(my_dp + j, dp), me), device_id_type=MESH
        )
        return c

    lax.fori_loop(1, n, greet, 0)
    lax.fori_loop(1, dp, greet_dp, 0)
    pl.semaphore_wait(barrier, n - 1 + dp - 1)

    def lanes(i):
        return pl.ds(pl.multiple_of(i * HD, HD), HD)

    def remote(src, dst, send, recv, target):
        pltpu.make_async_remote_copy(
            src_ref=src, dst_ref=dst, send_sem=send, recv_sem=recv,
            device_id=(my_dp, target), device_id_type=MESH,
        ).start()

    def move(src, dst, send, recv, target):
        @pl.when(target == me)
        def _():
            pltpu.make_async_copy(src, dst, recv).start()

        @pl.when(target != me)
        def _():
            remote(src, dst, send, recv, target)

    def wait_for(ref, sem):
        pltpu.make_async_copy(ref, ref, sem).wait()

    def kv_head(group, to):
        first = 2 * lax.rem(to // 2, 2) + lax.rem(to, 2)
        second = 4 + 2 * (to // 4) + lax.rem(to, 2)
        return first if group == 0 else second

    mine = rows(me, tok)

    def send_kv(group):
        def one(j, c):
            to = lax.rem(me + j, n)
            last = 2 * (to // 4) + 1 if group == 0 else 2 + lax.rem(to // 2, 2)

            @pl.when(chip <= last)
            def _():
                col = lanes(kv_head(group, to))
                move(k_in.at[0, :, col], k_all.at[group, mine], send_sem.at[group],
                     k_sem.at[group * 4 + chip], to)
                move(v_in.at[0, :, col], v_all.at[group, mine], send_sem.at[2 + group],
                     v_sem.at[group * 4 + chip], to)

            return c

        lax.fori_loop(0, n, one, 0)

    def send_q(group, m):
        item = 2 * m + group
        slot = x if group == 0 else y
        place = rows(2 * slot + core, tok)

        def one(j, c):
            far = lax.rem((x if group == 0 else y) + j // 2, 2)
            to = 2 * far + lax.rem(core + j, 2) + (4 * y if group == 0 else 0)
            if group == 1:
                to = 4 * far + 2 * x + lax.rem(core + j, 2)
            col = lanes(kv_head(group, to) * per + m)
            at = item * 2 + slot
            move(q_in.at[0, :, col], q_all.at[item, place], send_sem.at[4], q_sem.at[at], to)
            move(g_in.at[0, :, col], g_all.at[item, place], send_sem.at[5], g_sem.at[at], to)
            return c

        lax.fori_loop(0, 4, one, 0)

    send_kv(0)
    send_q(0, 0)
    send_kv(1)
    send_q(1, 0)

    z_own[...] = jnp.zeros_like(z_own)
    dk_acc[...] = jnp.zeros_like(dk_acc)
    dv_acc[...] = jnp.zeros_like(dv_acc)
    first_half = lax.broadcasted_iota(jnp.int32, (1, TILE), 1) < BLK
    causal = lax.broadcasted_iota(jnp.int32, (TILE, TILE), 0) <= lax.broadcasted_iota(
        jnp.int32, (TILE, TILE), 1
    )

    def prepare(group, last):
        def one(c, carry):
            at = rows(c, TILE)
            wait_for(k_all.at[group, at], k_sem.at[group * 4 + c])
            wait_for(v_all.at[group, at], v_sem.at[group * 4 + c])
            k_tr[group, :, at] = k_all[group, at, :].astype(jnp.float32).T.astype(jnp.bfloat16)
            v_tr[group, :, at] = v_all[group, at, :].astype(jnp.float32).T.astype(jnp.bfloat16)
            return carry

        lax.fori_loop(0, last + 1, one, 0)

    def tile_pair(pair, group, head, item):
        work = []
        for slot, t in ((1, pair[1]), (0, pair[0])):
            q = q_all[item, rows(slot, TILE), :]
            g = g_all[item, rows(slot, TILE), :]
            g_f32 = g.astype(jnp.float32).T
            work.append(dict(
                slot=slot, t=t, span=pl.ds(0, (t + 1) * TILE), q=q, g=g, g_f32=g_f32,
                q_tr=q.astype(jnp.float32).T.astype(jnp.bfloat16), g_tr=g_f32.astype(jnp.bfloat16),
            ))

        def bias(t, block):
            left = mask[2 * t, block, head]
            right = mask[2 * t + 1, block, head]
            on = jnp.where(first_half, left, right).astype(jnp.float32)
            return (1.0 - on) * NEG

        for w in work:
            t, slot = w["t"], w["slot"]
            top = jnp.full((8, TILE), NEG, jnp.float32)
            w["bias"] = [bias(t, block) for block in range(2 * t + 2)]
            for c in range(t + 1):
                at = rows(c, TILE)
                raw = dot(k_all[group, at, :], w["q_tr"])
                if c == t:
                    raw = jnp.where(causal, raw, NEG)
                score[slot, at, :] = raw
                for b in range(2):
                    best = fold(raw[b * BLK:(b + 1) * BLK], jnp.max) * (scale * LOG2E)
                    top = jnp.maximum(top, best + w["bias"][2 * c + b])
            w["top"] = jnp.max(top, axis=0, keepdims=True)
        for w in work:
            t, slot = w["t"], w["slot"]
            total = jnp.zeros((8, TILE), jnp.float32)
            for block in range(2 * t + 2):
                at = rows(block, BLK)
                e = jnp.exp2(
                    score[slot, at, :] * (scale * LOG2E) + (w["bias"][block] - w["top"])
                )
                score[slot, at, :] = e
                p_low[slot, at, :] = e.astype(jnp.bfloat16)
                total = total + fold(e, jnp.sum)
            w["total"] = jnp.sum(total, axis=0, keepdims=True)
            w["out"] = dot(v_tr[group, :, w["span"]], p_low[slot, w["span"], :])
        square = jnp.zeros((1, TILE), jnp.float32)
        for w in work:
            t, slot = w["t"], w["slot"]
            inverse = 1.0 / w["total"]
            out = (w["out"] * inverse).astype(jnp.bfloat16).astype(jnp.float32)
            delta = jnp.sum(w["g_f32"] * out, axis=0, keepdims=True)
            log_norm = w["top"] * LN2 + jnp.log(w["total"])
            shift = delta - (2.0 * ZLOSS) * log_norm
            square = square + log_norm * log_norm
            for c in range(t + 1):
                at = rows(c, TILE)
                p = score[slot, at, :] * inverse
                ds = p * (dot(v_all[group, at, :], w["g_tr"]) - shift)
                p_low[slot, at, :] = p.astype(jnp.bfloat16)
                ds_low[slot, at, :] = ds.astype(jnp.bfloat16)
        for w in work:
            slot, span = w["slot"], w["span"]
            dv_acc[group, span, :] += dot(p_low[slot, span, :], w["g"])
            dk_acc[group, span, :] += dot(ds_low[slot, span, :], w["q"])
            dq = dot(k_tr[group, :, span], ds_low[slot, span, :])
            dq_buf[item, rows(slot, TILE), :] = (dq * scale).T.astype(jnp.bfloat16)
        z_own[group, pl.ds(lax.rem(head, per), 1), :] += square[:, :BLK] + square[:, BLK:]

    def one_item(group, m):
        item = 2 * m + group
        half = y if group == 0 else x
        head_kv = kv_head(group, me)
        head = head_kv * per + m
        low = 2 * y if group == 0 else x
        high = 2 * y + 1 if group == 0 else 2 + x

        @pl.when(m == 0)
        def _():
            prepare(group, high)

        for slot in range(2):
            wait_for(q_all.at[item, rows(slot, TILE)], q_sem.at[item * 2 + slot])
            wait_for(g_all.at[item, rows(slot, TILE)], g_sem.at[item * 2 + slot])
        for choice, pair in enumerate(((0, 1), (2, 3)) if group == 0 else ((0, 2), (1, 3))):
            @pl.when(half == choice)
            def _(pair=pair):
                tile_pair(pair, group, head, item)

        def give_dq(i, c):
            tile = jnp.where(i < 2, high, low)
            part = lax.rem(i, 2)
            slot = 1 - i // 2
            move(dq_buf.at[item, rows(2 * slot + part, tok)], dq_out.at[0, :, lanes(head)],
                 send_sem.at[6], dq_sem.at[0], 2 * tile + part)
            return c

        lax.fori_loop(0, 4, give_dq, 0)

        @pl.when(m == per - 1)
        def _():
            sem = group * 2 + half
            col = lanes(head_kv)

            def give(c, carry):
                keys_at = rows(c, TILE)
                dk_buf[group, keys_at, :] = (dk_acc[group, keys_at, :] * scale).astype(jnp.bfloat16)
                dv_buf[group, keys_at, :] = dv_acc[group, keys_at, :].astype(jnp.bfloat16)
                for part in range(2):
                    to = 2 * c + part
                    move(dk_buf.at[group, rows(to, tok)], dk_part.at[half, :, col],
                         send_sem.at[7 + group], dk_sem.at[sem], to)
                    move(dv_buf.at[group, rows(to, tok)], dv_part.at[half, :, col],
                         send_sem.at[9 + group], dv_sem.at[sem], to)
                return carry

            lax.fori_loop(0, high + 1, give, 0)

    def one_step(m, carry):
        for group in range(2):
            @pl.when(m + 1 < per)
            def _(group=group):
                send_q(group, m + 1)

            one_item(group, m)
        return carry

    lax.fori_loop(0, per, one_step, 0)

    move(z_own.at[0], z_set.at[y], z_sem.at[0], z_sem.at[2 + y], kv_head(0, me))
    move(z_own.at[1], z_set.at[x], z_sem.at[1], z_sem.at[2 + x], kv_head(1, me))
    wait_for(z_set.at[0], z_sem.at[2])
    wait_for(z_set.at[1], z_sem.at[3])
    z_all[my_dp] = z_set[0] + z_set[1]

    def send_z(j, c):
        pltpu.make_async_remote_copy(
            src_ref=z_all.at[my_dp], dst_ref=z_all.at[my_dp],
            send_sem=z_sem.at[4], recv_sem=z_sem.at[5],
            device_id=(lax.rem(my_dp + j, dp), me), device_id_type=MESH,
        ).start()
        return c

    lax.fori_loop(1, dp, send_z, 0)
    wait_for(z_all.at[pl.ds(0, dp - 1)], z_sem.at[5])
    z_sum = jnp.sum(jnp.sum(z_all[...], axis=0), axis=1, keepdims=True)
    z_out[...] = jnp.broadcast_to(z_sum * (ZLOSS / (seq * dp)), z_out.shape)

    for group in range(2):
        cols = pl.ds(group * 4 * HD, 4 * HD)
        both = (y == 0) if group == 0 else (chip < 3)
        for part, sems, result in ((dk_part, dk_sem, dk_out), (dv_part, dv_sem, dv_out)):
            wait_for(part.at[1, :, cols], sems.at[group * 2 + 1])

            @pl.when(both)
            def _(part=part, sems=sems, result=result):
                wait_for(part.at[0, :, cols], sems.at[group * 2])
                result[0, :, cols] = (
                    part[0, :, cols].astype(jnp.float32) + part[1, :, cols].astype(jnp.float32)
                ).astype(jnp.bfloat16)

            @pl.when(jnp.logical_not(both))
            def _(part=part, result=result):
                result[0, :, cols] = part[1, :, cols]

    wait_for(dq_out, dq_sem.at[0])

    def sent(ref, sem, count):
        wait_for(ref.at[pl.ds(0, count * tok)], sem)

    for group in range(2):
        late = (y == 1) if group == 0 else (chip == 3)
        for sem in (group, 2 + group):
            @pl.when(late)
            def _(sem=sem):
                sent(k_all.at[0], send_sem.at[sem], 3)

            @pl.when(jnp.logical_not(late))
            def _(sem=sem):
                sent(k_all.at[0], send_sem.at[sem], 7)

        whole = (y == 1) if group == 0 else (x == 1)
        for sem in (7 + group, 9 + group):
            @pl.when(whole)
            def _(sem=sem):
                sent(k_all.at[0], send_sem.at[sem], 7)

            @pl.when(jnp.logical_not(whole))
            def _(sem=sem):
                sent(k_all.at[0], send_sem.at[sem], 3 if group == 0 else 5)

        @pl.when(kv_head(group, me) != me)
        def _():
            wait_for(z_own.at[group], z_sem.at[group])

    wide = pl.ds(0, 24 * HD)
    for sem in (4, 5, 6):
        wait_for(dq_out.at[0, :, wide], send_sem.at[sem])
    wait_for(z_all.at[pl.ds(0, dp - 1)], z_sem.at[4])


def finish_kernel(dq, dk, dv, z, dq_out, dk_out, dv_out, z_out, sem):
    copies = [
        pltpu.make_async_copy(a, b, sem.at[i])
        for i, (a, b) in enumerate(((dq, dq_out), (dk, dk_out), (dv, dv_out)))
    ]
    for copy in copies:
        copy.start()
    for h in range(z_out.shape[0]):
        z_out[h] = z[h, 0]
    for copy in copies:
        copy.wait()


def quad_body(queries, keys, values, out_grad, block_mask):
    dp = lax.axis_size("dp")
    seq, items = 8 * BLK, 8
    low, wide = jnp.bfloat16, jnp.float32
    hbm = pl.BlockSpec(memory_space=pltpu.HBM)
    vmem = pl.BlockSpec(memory_space=pltpu.VMEM)
    smem = pl.BlockSpec(memory_space=pltpu.SMEM)
    shape = jax.ShapeDtypeStruct
    results = pl.pallas_call(
        functools.partial(quad_kernel, dp),
        out_shape=(
            shape(queries.shape, low), shape(keys.shape, low), shape(keys.shape, low),
            shape((8, BLK), wide),
        ),
        in_specs=[smem] + [hbm] * 4,
        out_specs=(hbm, vmem, vmem, vmem),
        scratch_shapes=[
            pltpu.VMEM((items, 2 * TILE, HD), low),
            pltpu.VMEM((items, 2 * TILE, HD), low),
            pltpu.VMEM((2, seq, HD), low),
            pltpu.VMEM((2, seq, HD), low),
            pltpu.VMEM((2, HD, seq), low),
            pltpu.VMEM((2, HD, seq), low),
            pltpu.VMEM((2, seq, TILE), wide),
            pltpu.VMEM((2, seq, TILE), low),
            pltpu.VMEM((2, seq, TILE), low),
            pltpu.VMEM((2, seq, HD), wide),
            pltpu.VMEM((2, seq, HD), wide),
            pltpu.VMEM((items, 2 * TILE, HD), low),
            pltpu.VMEM((2, seq, HD), low),
            pltpu.VMEM((2, seq, HD), low),
            pltpu.VMEM((2, BLK, KVH * HD), low),
            pltpu.VMEM((2, BLK, KVH * HD), low),
            pltpu.VMEM((2, 8, BLK), wide),
            pltpu.VMEM((2, 8, BLK), wide),
            pltpu.VMEM((dp, 8, BLK), wide),
            pltpu.SemaphoreType.DMA((2 * items,)),
            pltpu.SemaphoreType.DMA((2 * items,)),
            pltpu.SemaphoreType.DMA((8,)),
            pltpu.SemaphoreType.DMA((8,)),
            pltpu.SemaphoreType.DMA((1,)),
            pltpu.SemaphoreType.DMA((4,)),
            pltpu.SemaphoreType.DMA((4,)),
            pltpu.SemaphoreType.DMA((11,)),
            pltpu.SemaphoreType.DMA((6,)),
        ],
        compiler_params=pltpu.CompilerParams(
            collective_id=0, has_side_effects=True, vmem_limit_bytes=60 * 1024 * 1024
        ),
        name="attention_exchange",
    )(block_mask.transpose(1, 2, 0), queries, out_grad, keys, values)
    return pl.pallas_call(
        finish_kernel,
        out_shape=(
            shape(queries.shape, low), shape(keys.shape, low), shape(keys.shape, low),
            shape((H // 8,), wide),
        ),
        in_specs=[vmem, vmem, vmem, smem],
        out_specs=(hbm, hbm, hbm, smem),
        scratch_shapes=[pltpu.SemaphoreType.DMA((3,))],
        compiler_params=pltpu.CompilerParams(vmem_limit_bytes=62 * 1024 * 1024),
        name="write_results",
    )(*results)


def solution(mesh):
    quad = mesh.shape["ctx"] == 8
    return jax.shard_map(
        quad_body if quad else body,
        mesh=mesh,
        in_specs=(
            P("dp", "ctx", None),
            P("dp", "ctx", None),
            P("dp", "ctx", None),
            P("dp", "ctx", None),
            P(),
        ),
        out_specs=(P("dp", "ctx", None), P("dp", "ctx", None), P("dp", "ctx", None), P("ctx")),
        check_vma=False,
    )
```

```python
import functools
import math

import jax
import jax.numpy as jnp
from jax import lax
from jax.experimental import pallas as pl
from jax.experimental.pallas import tpu as pltpu
from jax.sharding import PartitionSpec as P

H = 32
KVH = 8
HD = 128
BLK = 128
ZLOSS = 0.05
NEG = -1e30
TILE = 2 * BLK
MESH = pl.DeviceIdType.MESH
LOG2E = math.log2(math.e)
LN2 = math.log(2.0)


def dot(a, b):
    return jnp.dot(a, b, preferred_element_type=jnp.float32)


def steps(count, step, state):
    if isinstance(count, int) and count <= 4:
        for i in range(count):
            state = step(i, state)
        return state
    return lax.fori_loop(0, count, step, state)


def rows(i, size):
    return pl.ds(i * size if isinstance(i, int) else pl.multiple_of(i * size, size), size)


def fold(x, op):
    return op(x.reshape(x.shape[0] // 8, 8, x.shape[1]), axis=0)


def kernel(
    sizes,
    mask, q_in, g_in, k_in, v_in,
    dq_out, dk_out, dv_out, z_out,
    q_all, g_all, k_all, v_all, k_tr, v_tr,
    score, dk_acc, dv_acc, dq_buf, dk_buf, dv_buf, z_own, z_all,
    q_sem, g_sem, kv_sem, out_sem, send_sem, z_sem,
):
    n, dp, per, share, tok = sizes
    seq = n * tok
    tiles = seq // TILE
    me = lax.axis_index("ctx")
    my_dp = lax.axis_index("dp")
    group = H // KVH
    scale = HD ** (-0.5)

    barrier = pltpu.get_barrier_semaphore()

    def greet(j, c):
        pl.semaphore_signal(
            barrier, inc=1, device_id=(my_dp, lax.rem(me + j, n)), device_id_type=MESH
        )
        return c

    def greet_dp(j, c):
        pl.semaphore_signal(
            barrier, inc=1, device_id=(lax.rem(my_dp + j, dp), me), device_id_type=MESH
        )
        return c

    lax.fori_loop(1, n, greet, 0)
    lax.fori_loop(1, dp, greet_dp, 0)
    pl.semaphore_wait(barrier, n - 1 + dp - 1)

    def lanes(i):
        return pl.ds(pl.multiple_of(i * HD, HD), HD)

    def remote(src, dst, send, recv, target):
        pltpu.make_async_remote_copy(
            src_ref=src, dst_ref=dst, send_sem=send, recv_sem=recv,
            device_id=(my_dp, target), device_id_type=MESH,
        ).start()

    mine = rows(me, tok)

    def kv_head(device):
        return (device * per) // group

    def send_kv(j, c):
        to = lax.rem(me + j, n)
        col = lanes(kv_head(to))
        remote(k_in.at[0, :, col], k_all.at[mine], send_sem.at[0], kv_sem.at[0], to)
        remote(v_in.at[0, :, col], v_all.at[mine], send_sem.at[1], kv_sem.at[1], to)
        return c

    lax.fori_loop(1, n, send_kv, 0)
    own = lanes(kv_head(me))
    pltpu.make_async_copy(k_in.at[0, :, own], k_all.at[mine], kv_sem.at[0]).start()
    pltpu.make_async_copy(v_in.at[0, :, own], v_all.at[mine], kv_sem.at[1]).start()

    def send_head(h, c):
        def send_q(j, c):
            to = lax.rem(me + j, n)
            col = lanes(to * per + h)
            remote(q_in.at[0, :, col], q_all.at[h, mine], send_sem.at[2], q_sem.at[h], to)
            remote(g_in.at[0, :, col], g_all.at[h, mine], send_sem.at[3], g_sem.at[h], to)
            return c

        lax.fori_loop(1, n, send_q, 0)
        col = lanes(me * per + h)
        pltpu.make_async_copy(q_in.at[0, :, col], q_all.at[h, mine], q_sem.at[h]).start()
        pltpu.make_async_copy(g_in.at[0, :, col], g_all.at[h, mine], g_sem.at[h]).start()
        return c

    lax.fori_loop(0, per, send_head, 0)

    def wait_for(ref, sem):
        pltpu.make_async_copy(ref, ref, sem).wait()

    z_own[...] = jnp.zeros_like(z_own)
    dk_acc[...] = jnp.zeros_like(dk_acc)
    dv_acc[...] = jnp.zeros_like(dv_acc)
    wait_for(k_all, kv_sem.at[0])
    wait_for(v_all, kv_sem.at[1])

    def turn(c, s):
        at = rows(c, TILE)
        k_tr[:, at] = k_all[at].astype(jnp.float32).T.astype(jnp.bfloat16)
        v_tr[:, at] = v_all[at].astype(jnp.float32).T.astype(jnp.bfloat16)
        return s

    steps(tiles, turn, 0)
    first_half = lax.broadcasted_iota(jnp.int32, (1, TILE), 1) < BLK
    causal = lax.broadcasted_iota(jnp.int32, (TILE, TILE), 0) <= lax.broadcasted_iota(
        jnp.int32, (TILE, TILE), 1
    )

    def one_head(h, c):
        wait_for(q_all.at[h], q_sem.at[h])
        wait_for(g_all.at[h], g_sem.at[h])
        head = me * per + h

        def one_tile(t):
            q_at = rows(t, TILE)
            q = q_all[h, q_at, :]
            g = g_all[h, q_at, :]
            q_tr = q.astype(jnp.float32).T.astype(jnp.bfloat16)
            g_f32 = g.astype(jnp.float32).T
            g_tr = g_f32.astype(jnp.bfloat16)

            def bias(c):
                parts = []
                for b in range(2):
                    left = mask[2 * t, 2 * c + b, head]
                    right = mask[2 * t + 1, 2 * c + b, head]
                    on = jnp.where(first_half, left, right).astype(jnp.float32)
                    parts.append(jnp.broadcast_to((1.0 - on) * NEG, (BLK, TILE)))
                return jnp.concatenate(parts, axis=0)

            def score_chunk(c, top, diagonal):
                at = rows(c, TILE)
                s = dot(k_all[at], q_tr) * (scale * LOG2E) + bias(c)
                if diagonal:
                    s = jnp.where(causal, s, NEG)
                score[at] = s
                return jnp.maximum(top, fold(s, jnp.max))

            top = jnp.full((8, TILE), NEG, jnp.float32)
            top = steps(t, lambda c, x: score_chunk(c, x, False), top)
            top = score_chunk(t, top, True)
            top = jnp.max(top, axis=0, keepdims=True)

            def exp_chunk(c, state):
                total, out = state
                at = rows(c, TILE)
                e = jnp.exp2(score[at] - top)
                score[at] = e
                out = out + dot(v_tr[:, at], e.astype(jnp.bfloat16))
                return total + fold(e, jnp.sum), out

            total, out = steps(
                t + 1, exp_chunk,
                (jnp.zeros((8, TILE), jnp.float32), jnp.zeros((HD, TILE), jnp.float32)),
            )
            total = jnp.sum(total, axis=0, keepdims=True)
            inverse = 1.0 / total
            out = (out * inverse).astype(jnp.bfloat16).astype(jnp.float32)
            delta = jnp.sum(g_f32 * out, axis=0, keepdims=True)
            log_norm = top * LN2 + jnp.log(total)
            shift = delta - (2.0 * ZLOSS) * log_norm
            square = log_norm * log_norm
            z_own[pl.ds(h, 1), :] += square[:, :BLK] + square[:, BLK:]

            def grad_chunk(c, dq):
                at = rows(c, TILE)
                p = score[at] * inverse
                dv_acc[at] += dot(p.astype(jnp.bfloat16), g)
                ds = (p * (dot(v_all[at], g_tr) - shift)).astype(jnp.bfloat16)
                dk_acc[at] += dot(ds, q)
                return dq + dot(k_tr[:, at], ds)

            dq = steps(t + 1, grad_chunk, jnp.zeros((HD, TILE), jnp.float32))
            dq_buf[h, q_at, :] = (dq * scale).T.astype(jnp.bfloat16)

            for part in range(TILE // tok):
                to = t * (TILE // tok) + part
                src = dq_buf.at[h, rows(to, tok)]
                dst = dq_out.at[0, :, lanes(head)]

                @pl.when(me == to)
                def _():
                    pltpu.make_async_copy(src, dst, out_sem.at[0]).start()

                @pl.when(me != to)
                def _():
                    remote(src, dst, send_sem.at[4], out_sem.at[0], to)

            @pl.when(h == per - 1)
            def _():
                dk_buf[q_at] = (dk_acc[q_at] * scale).astype(jnp.bfloat16)
                dv_buf[q_at] = dv_acc[q_at].astype(jnp.bfloat16)
                slot = lax.rem(me, share)
                col = lanes(kv_head(me))
                for part in range(TILE // tok):
                    to = t * (TILE // tok) + part
                    src_k = dk_buf.at[rows(to, tok)]
                    src_v = dv_buf.at[rows(to, tok)]

                    @pl.when(me == to)
                    def _():
                        pltpu.make_async_copy(src_k, dk_out.at[slot, :, col], out_sem.at[1]).start()
                        pltpu.make_async_copy(src_v, dv_out.at[slot, :, col], out_sem.at[2]).start()

                    @pl.when(me != to)
                    def _():
                        remote(src_k, dk_out.at[slot, :, col], send_sem.at[5], out_sem.at[1], to)
                        remote(src_v, dv_out.at[slot, :, col], send_sem.at[6], out_sem.at[2], to)

        if tiles <= 4:
            for t in reversed(range(tiles)):
                one_tile(t)
        else:
            def tile_step(i, s):
                one_tile(tiles - 1 - i)
                return s

            lax.fori_loop(0, tiles, tile_step, 0)
        return c

    lax.fori_loop(0, per, one_head, 0)

    pltpu.make_async_copy(z_own, z_all.at[my_dp], z_sem.at[1]).start()

    def send_z(j, c):
        pltpu.make_async_remote_copy(
            src_ref=z_own, dst_ref=z_all.at[my_dp], send_sem=z_sem.at[0], recv_sem=z_sem.at[1],
            device_id=(lax.rem(my_dp + j, dp), me), device_id_type=MESH,
        ).start()
        return c

    lax.fori_loop(1, dp, send_z, 0)
    wait_for(z_all, z_sem.at[1])
    z_sum = jnp.sum(jnp.sum(z_all[...], axis=0), axis=1, keepdims=True)
    z_out[...] = jnp.broadcast_to(z_sum * (ZLOSS / (seq * dp)), z_out.shape)

    wait_for(dq_out, out_sem.at[0])
    wait_for(dk_out, out_sem.at[1])
    wait_for(dv_out, out_sem.at[2])
    others = pl.ds(0, seq - tok)
    wide = pl.ds(0, (n - 1) * per * HD)
    wait_for(k_all.at[others], send_sem.at[0])
    wait_for(v_all.at[others], send_sem.at[1])
    wait_for(q_in.at[0, :, wide], send_sem.at[2])
    wait_for(g_in.at[0, :, wide], send_sem.at[3])
    wait_for(dq_out.at[0, :, wide], send_sem.at[4])
    wait_for(dk_buf.at[others], send_sem.at[5])
    wait_for(dv_buf.at[others], send_sem.at[6])
    wait_for(z_all.at[pl.ds(0, dp - 1)], z_sem.at[0])


def body(queries, keys, values, out_grad, block_mask):
    tok = queries.shape[1]
    n = lax.axis_size("ctx")
    dp = lax.axis_size("dp")
    per = H // n
    share = max(1, n // KVH)
    seq = tok * n
    low, wide = jnp.bfloat16, jnp.float32
    anywhere = pl.BlockSpec(memory_space=pl.ANY)
    dq, dk, dv, z = pl.pallas_call(
        functools.partial(kernel, (n, dp, per, share, tok)),
        out_shape=(
            jax.ShapeDtypeStruct(queries.shape, low),
            jax.ShapeDtypeStruct((share, tok, KVH * HD), low),
            jax.ShapeDtypeStruct((share, tok, KVH * HD), low),
            jax.ShapeDtypeStruct((8, BLK), wide),
        ),
        in_specs=[pl.BlockSpec(memory_space=pltpu.SMEM)] + [anywhere] * 4,
        out_specs=(anywhere, anywhere, anywhere, pl.BlockSpec(memory_space=pltpu.VMEM)),
        scratch_shapes=[
            pltpu.VMEM((per, seq, HD), low),
            pltpu.VMEM((per, seq, HD), low),
            pltpu.VMEM((seq, HD), low),
            pltpu.VMEM((seq, HD), low),
            pltpu.VMEM((HD, seq), low),
            pltpu.VMEM((HD, seq), low),
            pltpu.VMEM((seq, TILE), wide),
            pltpu.VMEM((seq, HD), wide),
            pltpu.VMEM((seq, HD), wide),
            pltpu.VMEM((per, seq, HD), low),
            pltpu.VMEM((seq, HD), low),
            pltpu.VMEM((seq, HD), low),
            pltpu.VMEM((8, BLK), wide),
            pltpu.VMEM((dp, 8, BLK), wide),
            pltpu.SemaphoreType.DMA((per,)),
            pltpu.SemaphoreType.DMA((per,)),
            pltpu.SemaphoreType.DMA((2,)),
            pltpu.SemaphoreType.DMA((3,)),
            pltpu.SemaphoreType.DMA((7,)),
            pltpu.SemaphoreType.DMA((2,)),
        ],
        compiler_params=pltpu.CompilerParams(
            collective_id=0, has_side_effects=True, vmem_limit_bytes=62 * 1024 * 1024
        ),
        name="attention_exchange",
    )(block_mask.transpose(1, 2, 0), queries, out_grad, keys, values)
    if share > 1:
        dk = jnp.sum(dk.astype(wide), axis=0, keepdims=True).astype(low)
        dv = jnp.sum(dv.astype(wide), axis=0, keepdims=True).astype(low)
    return (dq, dk, dv, z[:per, 0])


def quad_kernel(
    dp,
    mask, q_in, g_in, k_in, v_in,
    dq_out, dk_out, dv_out, z_out,
    q_all, g_all, k_all, v_all, k_tr, v_tr,
    score, p_low, ds_low, dk_acc, dv_acc, dq_buf, dk_buf, dv_buf, dk_part, dv_part, z_own, z_set, z_all,
    q_sem, g_sem, k_sem, v_sem, dq_sem, dk_sem, dv_sem, send_sem, z_sem,
):
    n, tok, per = 8, BLK, H // KVH
    seq = n * tok
    me = lax.axis_index("ctx")
    my_dp = lax.axis_index("dp")
    y, x, core = me // 4, lax.rem(me // 2, 2), lax.rem(me, 2)
    chip = me // 2
    scale = HD ** (-0.5)

    barrier = pltpu.get_barrier_semaphore()

    def greet(j, c):
        pl.semaphore_signal(
            barrier, inc=1, device_id=(my_dp, lax.rem(me + j, n)), device_id_type=MESH
        )
        return c

    def greet_dp(j, c):
        pl.semaphore_signal(
            barrier, inc=1, device_id=(lax.rem(my_dp + j, dp), me), device_id_type=MESH
        )
        return c

    lax.fori_loop(1, n, greet, 0)
    lax.fori_loop(1, dp, greet_dp, 0)
    pl.semaphore_wait(barrier, n - 1 + dp - 1)

    def lanes(i):
        return pl.ds(pl.multiple_of(i * HD, HD), HD)

    def remote(src, dst, send, recv, target):
        pltpu.make_async_remote_copy(
            src_ref=src, dst_ref=dst, send_sem=send, recv_sem=recv,
            device_id=(my_dp, target), device_id_type=MESH,
        ).start()

    def move(src, dst, send, recv, target):
        @pl.when(target == me)
        def _():
            pltpu.make_async_copy(src, dst, recv).start()

        @pl.when(target != me)
        def _():
            remote(src, dst, send, recv, target)

    def wait_for(ref, sem):
        pltpu.make_async_copy(ref, ref, sem).wait()

    def kv_head(group, to):
        first = 2 * lax.rem(to // 2, 2) + lax.rem(to, 2)
        second = 4 + 2 * (to // 4) + lax.rem(to, 2)
        return first if group == 0 else second

    mine = rows(me, tok)

    def send_kv(group):
        def one(j, c):
            to = lax.rem(me + j, n)
            last = 2 * (to // 4) + 1 if group == 0 else 2 + lax.rem(to // 2, 2)

            @pl.when(chip <= last)
            def _():
                col = lanes(kv_head(group, to))
                move(k_in.at[0, :, col], k_all.at[group, mine], send_sem.at[group],
                     k_sem.at[group * 4 + chip], to)
                move(v_in.at[0, :, col], v_all.at[group, mine], send_sem.at[2 + group],
                     v_sem.at[group * 4 + chip], to)

            return c

        lax.fori_loop(0, n, one, 0)

    pieces = (pl.ds(0, HD), pl.ds(HD, (per - 1) * HD))

    def send_q(group, piece):
        slot = x if group == 0 else y
        place = rows(2 * slot + core, tok)

        def one(j, c):
            far = lax.rem((x if group == 0 else y) + j // 2, 2)
            to = 2 * far + lax.rem(core + j, 2) + (4 * y if group == 0 else 0)
            if group == 1:
                to = 4 * far + 2 * x + lax.rem(core + j, 2)
            first = pl.multiple_of((kv_head(group, to) * per + piece) * HD, HD)
            col, put = pl.ds(first, pieces[piece].size), pieces[piece]
            at = (group * 2 + slot) * 2 + piece
            move(q_in.at[0, :, col], q_all.at[group, place, put], send_sem.at[4], q_sem.at[at], to)
            move(g_in.at[0, :, col], g_all.at[group, place, put], send_sem.at[5], g_sem.at[at], to)
            return c

        lax.fori_loop(0, 4, one, 0)

    send_kv(0)
    send_q(0, 0)
    send_kv(1)
    send_q(1, 0)
    send_q(0, 1)
    send_q(1, 1)

    z_own[...] = jnp.zeros_like(z_own)
    dk_acc[...] = jnp.zeros_like(dk_acc)
    dv_acc[...] = jnp.zeros_like(dv_acc)
    first_half = lax.broadcasted_iota(jnp.int32, (1, TILE), 1) < BLK
    causal = lax.broadcasted_iota(jnp.int32, (TILE, TILE), 0) <= lax.broadcasted_iota(
        jnp.int32, (TILE, TILE), 1
    )

    def prepare(group, last):
        def one(c, carry):
            at = rows(c, TILE)
            wait_for(k_all.at[group, at], k_sem.at[group * 4 + c])
            wait_for(v_all.at[group, at], v_sem.at[group * 4 + c])
            k_tr[group, :, at] = k_all[group, at, :].astype(jnp.float32).T.astype(jnp.bfloat16)
            v_tr[group, :, at] = v_all[group, at, :].astype(jnp.float32).T.astype(jnp.bfloat16)
            return carry

        lax.fori_loop(0, last + 1, one, 0)

    def tile_pair(pair, group, head, item):
        work = []
        for slot, t in ((1, pair[1]), (0, pair[0])):
            q = q_all[group, rows(slot, TILE), lanes(item // 2)]
            g = g_all[group, rows(slot, TILE), lanes(item // 2)]
            g_f32 = g.astype(jnp.float32).T
            work.append(dict(
                slot=slot, t=t, span=pl.ds(0, (t + 1) * TILE), q=q, g=g, g_f32=g_f32,
                q_tr=q.astype(jnp.float32).T.astype(jnp.bfloat16), g_tr=g_f32.astype(jnp.bfloat16),
            ))

        def bias(t, block):
            left = mask[2 * t, block, head]
            right = mask[2 * t + 1, block, head]
            on = jnp.where(first_half, left, right).astype(jnp.float32)
            return (1.0 - on) * NEG

        for w in work:
            t, slot = w["t"], w["slot"]
            top = jnp.full((8, TILE), NEG, jnp.float32)
            w["bias"] = [bias(t, block) for block in range(2 * t + 2)]
            for c in range(t + 1):
                at = rows(c, TILE)
                raw = dot(k_all[group, at, :], w["q_tr"])
                if c == t:
                    raw = jnp.where(causal, raw, NEG)
                score[slot, at, :] = raw
                for b in range(2):
                    best = fold(raw[b * BLK:(b + 1) * BLK], jnp.max) * (scale * LOG2E)
                    top = jnp.maximum(top, best + w["bias"][2 * c + b])
            w["top"] = jnp.max(top, axis=0, keepdims=True)
        for w in work:
            t, slot = w["t"], w["slot"]
            total = jnp.zeros((8, TILE), jnp.float32)
            for block in range(2 * t + 2):
                at = rows(block, BLK)
                e = jnp.exp2(
                    score[slot, at, :] * (scale * LOG2E) + (w["bias"][block] - w["top"])
                )
                score[slot, at, :] = e
                p_low[slot, at, :] = e.astype(jnp.bfloat16)
                total = total + fold(e, jnp.sum)
            w["total"] = jnp.sum(total, axis=0, keepdims=True)
            w["out"] = dot(v_tr[group, :, w["span"]], p_low[slot, w["span"], :])
        square = jnp.zeros((1, TILE), jnp.float32)
        for w in work:
            t, slot = w["t"], w["slot"]
            inverse = 1.0 / w["total"]
            out = (w["out"] * inverse).astype(jnp.bfloat16).astype(jnp.float32)
            delta = jnp.sum(w["g_f32"] * out, axis=0, keepdims=True)
            log_norm = w["top"] * LN2 + jnp.log(w["total"])
            shift = delta - (2.0 * ZLOSS) * log_norm
            square = square + log_norm * log_norm
            for c in range(t + 1):
                at = rows(c, TILE)
                p = score[slot, at, :] * inverse
                ds = p * (dot(v_all[group, at, :], w["g_tr"]) - shift)
                p_low[slot, at, :] = p.astype(jnp.bfloat16)
                ds_low[slot, at, :] = ds.astype(jnp.bfloat16)
        for w in work:
            slot, span = w["slot"], w["span"]
            dv_acc[group, span, :] += dot(p_low[slot, span, :], w["g"])
            dk_acc[group, span, :] += dot(ds_low[slot, span, :], w["q"])
            dq = dot(k_tr[group, :, span], ds_low[slot, span, :])
            dq_buf[item, rows(slot, TILE), :] = (dq * scale).T.astype(jnp.bfloat16)
        z_own[group, pl.ds(lax.rem(head, per), 1), :] += square[:, :BLK] + square[:, BLK:]

    def one_item(group, m):
        item = 2 * m + group
        half = y if group == 0 else x
        head_kv = kv_head(group, me)
        head = head_kv * per + m
        low = 2 * y if group == 0 else x
        high = 2 * y + 1 if group == 0 else 2 + x

        @pl.when(m == 0)
        def _():
            prepare(group, high)

        for piece in range(2):
            @pl.when(m == piece)
            def _(piece=piece):
                for slot in range(2):
                    place, at = rows(slot, TILE), (group * 2 + slot) * 2 + piece
                    wait_for(q_all.at[group, place, pieces[piece]], q_sem.at[at])
                    wait_for(g_all.at[group, place, pieces[piece]], g_sem.at[at])

        for choice, pair in enumerate(((0, 1), (2, 3)) if group == 0 else ((0, 2), (1, 3))):
            @pl.when(half == choice)
            def _(pair=pair):
                tile_pair(pair, group, head, item)

        def give_dq(i, c):
            tile = jnp.where(i < 2, high, low)
            part = lax.rem(i, 2)
            slot = 1 - i // 2
            move(dq_buf.at[item, rows(2 * slot + part, tok)], dq_out.at[0, :, lanes(head)],
                 send_sem.at[6], dq_sem.at[0], 2 * tile + part)
            return c

        lax.fori_loop(0, 4, give_dq, 0)

        @pl.when(m == per - 1)
        def _():
            sem = group * 2 + half
            col = lanes(head_kv)

            def give(c, carry):
                keys_at = rows(c, TILE)
                dk_buf[group, keys_at, :] = (dk_acc[group, keys_at, :] * scale).astype(jnp.bfloat16)
                dv_buf[group, keys_at, :] = dv_acc[group, keys_at, :].astype(jnp.bfloat16)
                for part in range(2):
                    to = 2 * c + part
                    move(dk_buf.at[group, rows(to, tok)], dk_part.at[half, :, col],
                         send_sem.at[7 + group], dk_sem.at[sem], to)
                    move(dv_buf.at[group, rows(to, tok)], dv_part.at[half, :, col],
                         send_sem.at[9 + group], dv_sem.at[sem], to)
                return carry

            lax.fori_loop(0, high + 1, give, 0)

    def one_step(m, carry):
        one_item(0, m)
        one_item(1, m)
        return carry

    lax.fori_loop(0, per, one_step, 0)

    move(z_own.at[0], z_set.at[y], z_sem.at[0], z_sem.at[2 + y], kv_head(0, me))
    move(z_own.at[1], z_set.at[x], z_sem.at[1], z_sem.at[2 + x], kv_head(1, me))
    wait_for(z_set.at[0], z_sem.at[2])
    wait_for(z_set.at[1], z_sem.at[3])
    z_all[my_dp] = z_set[0] + z_set[1]

    def send_z(j, c):
        pltpu.make_async_remote_copy(
            src_ref=z_all.at[my_dp], dst_ref=z_all.at[my_dp],
            send_sem=z_sem.at[4], recv_sem=z_sem.at[5],
            device_id=(lax.rem(my_dp + j, dp), me), device_id_type=MESH,
        ).start()
        return c

    lax.fori_loop(1, dp, send_z, 0)
    wait_for(z_all.at[pl.ds(0, dp - 1)], z_sem.at[5])
    z_sum = jnp.sum(jnp.sum(z_all[...], axis=0), axis=1, keepdims=True)
    z_out[...] = jnp.broadcast_to(z_sum * (ZLOSS / (seq * dp)), z_out.shape)

    for group in range(2):
        cols = pl.ds(group * 4 * HD, 4 * HD)
        both = (y == 0) if group == 0 else (chip < 3)
        for part, sems, result in ((dk_part, dk_sem, dk_out), (dv_part, dv_sem, dv_out)):
            wait_for(part.at[1, :, cols], sems.at[group * 2 + 1])

            @pl.when(both)
            def _(part=part, sems=sems, result=result):
                wait_for(part.at[0, :, cols], sems.at[group * 2])
                result[0, :, cols] = (
                    part[0, :, cols].astype(jnp.float32) + part[1, :, cols].astype(jnp.float32)
                ).astype(jnp.bfloat16)

            @pl.when(jnp.logical_not(both))
            def _(part=part, result=result):
                result[0, :, cols] = part[1, :, cols]

    wait_for(dq_out, dq_sem.at[0])

    def sent(ref, sem, count):
        wait_for(ref.at[pl.ds(0, count * tok)], sem)

    for group in range(2):
        late = (y == 1) if group == 0 else (chip == 3)
        for sem in (group, 2 + group):
            @pl.when(late)
            def _(sem=sem):
                sent(k_all.at[0], send_sem.at[sem], 3)

            @pl.when(jnp.logical_not(late))
            def _(sem=sem):
                sent(k_all.at[0], send_sem.at[sem], 7)

        whole = (y == 1) if group == 0 else (x == 1)
        for sem in (7 + group, 9 + group):
            @pl.when(whole)
            def _(sem=sem):
                sent(k_all.at[0], send_sem.at[sem], 7)

            @pl.when(jnp.logical_not(whole))
            def _(sem=sem):
                sent(k_all.at[0], send_sem.at[sem], 3 if group == 0 else 5)

        @pl.when(kv_head(group, me) != me)
        def _():
            wait_for(z_own.at[group], z_sem.at[group])

    wide = pl.ds(0, 24 * HD)
    for sem in (4, 5, 6):
        wait_for(dq_out.at[0, :, wide], send_sem.at[sem])
    wait_for(z_all.at[pl.ds(0, dp - 1)], z_sem.at[4])


def finish_kernel(dq, dk, dv, z, dq_out, dk_out, dv_out, z_out, sem):
    copies = [
        pltpu.make_async_copy(a, b, sem.at[i])
        for i, (a, b) in enumerate(((dq, dq_out), (dk, dk_out), (dv, dv_out)))
    ]
    for copy in copies:
        copy.start()
    for h in range(z_out.shape[0]):
        z_out[h] = z[h, 0]
    for copy in copies:
        copy.wait()


def quad_body(queries, keys, values, out_grad, block_mask):
    dp = lax.axis_size("dp")
    seq, items = 8 * BLK, 8
    low, wide = jnp.bfloat16, jnp.float32
    hbm = pl.BlockSpec(memory_space=pltpu.HBM)
    vmem = pl.BlockSpec(memory_space=pltpu.VMEM)
    smem = pl.BlockSpec(memory_space=pltpu.SMEM)
    shape = jax.ShapeDtypeStruct
    results = pl.pallas_call(
        functools.partial(quad_kernel, dp),
        out_shape=(
            shape(queries.shape, low), shape(keys.shape, low), shape(keys.shape, low),
            shape((8, BLK), wide),
        ),
        in_specs=[smem] + [hbm] * 4,
        out_specs=(hbm, vmem, vmem, vmem),
        scratch_shapes=[
            pltpu.VMEM((2, 2 * TILE, items // 2 * HD), low),
            pltpu.VMEM((2, 2 * TILE, items // 2 * HD), low),
            pltpu.VMEM((2, seq, HD), low),
            pltpu.VMEM((2, seq, HD), low),
            pltpu.VMEM((2, HD, seq), low),
            pltpu.VMEM((2, HD, seq), low),
            pltpu.VMEM((2, seq, TILE), wide),
            pltpu.VMEM((2, seq, TILE), low),
            pltpu.VMEM((2, seq, TILE), low),
            pltpu.VMEM((2, seq, HD), wide),
            pltpu.VMEM((2, seq, HD), wide),
            pltpu.VMEM((items, 2 * TILE, HD), low),
            pltpu.VMEM((2, seq, HD), low),
            pltpu.VMEM((2, seq, HD), low),
            pltpu.VMEM((2, BLK, KVH * HD), low),
            pltpu.VMEM((2, BLK, KVH * HD), low),
            pltpu.VMEM((2, 8, BLK), wide),
            pltpu.VMEM((2, 8, BLK), wide),
            pltpu.VMEM((dp, 8, BLK), wide),
            pltpu.SemaphoreType.DMA((items,)),
            pltpu.SemaphoreType.DMA((items,)),
            pltpu.SemaphoreType.DMA((8,)),
            pltpu.SemaphoreType.DMA((8,)),
            pltpu.SemaphoreType.DMA((1,)),
            pltpu.SemaphoreType.DMA((4,)),
            pltpu.SemaphoreType.DMA((4,)),
            pltpu.SemaphoreType.DMA((11,)),
            pltpu.SemaphoreType.DMA((6,)),
        ],
        compiler_params=pltpu.CompilerParams(
            collective_id=0, has_side_effects=True, vmem_limit_bytes=60 * 1024 * 1024
        ),
        name="attention_exchange",
    )(block_mask.transpose(1, 2, 0), queries, out_grad, keys, values)
    return pl.pallas_call(
        finish_kernel,
        out_shape=(
            shape(queries.shape, low), shape(keys.shape, low), shape(keys.shape, low),
            shape((H // 8,), wide),
        ),
        in_specs=[vmem, vmem, vmem, smem],
        out_specs=(hbm, hbm, hbm, smem),
        scratch_shapes=[pltpu.SemaphoreType.DMA((3,))],
        compiler_params=pltpu.CompilerParams(vmem_limit_bytes=62 * 1024 * 1024),
        name="write_results",
    )(*results)


def solution(mesh):
    quad = mesh.shape["ctx"] == 8
    return jax.shard_map(
        quad_body if quad else body,
        mesh=mesh,
        in_specs=(
            P("dp", "ctx", None),
            P("dp", "ctx", None),
            P("dp", "ctx", None),
            P("dp", "ctx", None),
            P(),
        ),
        out_specs=(P("dp", "ctx", None), P("dp", "ctx", None), P("dp", "ctx", None), P("ctx")),
        check_vma=False,
    )
```
